32 devices in a mesh: win: 2 (over y), row: 16 (over z, x, core).
Axes of the slice: x: 2, y: 2, z: 4, core: 2. Of those that a mesh axis runs over, the one named last changes fastest.
Arguments:
- contact_map: bfloat16 [256, 128, 128], P(('win', 'row')), parts along dimension 0, may hold values from -6 to 6
- first_kernel: bfloat16 [3, 3, 128, 128], replicated, may hold values from -0.25 to 0.25
- second_kernel: bfloat16 [3, 3, 128, 128], replicated, may hold values from -0.25 to 0.25
- project_weight: bfloat16 [128, 128], replicated, may hold values from -0.75 to 0.75
Outputs:
- block_out: bfloat16 [256, 128, 128], P(('win', 'row')), parts along dimension 0
The draws below stay inside these ranges and needn't reach their ends.
There are 2 independent parts, one for each index of `win`. The reference program is written for one: setup_inputs(seed, part) draws one part's arguments, and reference() takes and returns one part's arrays. A program takes and returns all parts, laid end to end along the dimension named above; an argument that names none is the same for every part. Nothing has to cross between parts.
All inputs are finite; a program needn't handle non-finite values.
Results may differ from the reference program's by a relative error of at most 0.0055.
Values may be sent and summed in bfloat16 or wider, within the bound.
A program may use at most 64 MiB of HBM per device.

```python
import jax
import jax.numpy as jnp
from jax import lax

C = 128
L = 128


def steps_of(key, dims, cuts, least, largest):
    def one(dim, blocks):
        draws = jax.random.uniform(jax.random.fold_in(jax.random.fold_in(key, 6), dim), (blocks,), jnp.float32, least / len(cuts), largest / len(cuts))
        return jnp.repeat(jnp.exp(draws), dims[dim] // blocks).reshape((-1,) + (1,) * (len(dims) - dim - 1))

    gain = one(*cuts[0])
    for cut in cuts[1:]:
        gain = gain * one(*cut)
    return gain


def centred(key, extent, deviation, limit, cuts=(), dtype=jnp.bfloat16):
    array = deviation * jax.random.normal(key, extent, jnp.float32)
    if cuts:
        array = array * steps_of(key, extent, cuts, -0.22, 0.18)
    return jnp.clip(array, -limit, limit).astype(dtype)


def setup_inputs(seed: int = 0, part: int = 0) -> dict:
    key_of = jax.random.split(jax.random.key(seed), 5)
    own_keys = jax.random.split(jax.random.fold_in(key_of[4], part), 5)
    return {
        "contact_map": centred(own_keys[0], (L, L, C), 1.0, 6.0, ((0, 16),)),
        "first_kernel": centred(key_of[1], (3, 3, C, C), (9 * C // 2) ** -0.5, 0.25),
        "second_kernel": centred(key_of[2], (3, 3, C, C), (9 * C // 2) ** -0.5, 0.25),
        "project_weight": centred(key_of[3], (C, C), (C // 2) ** -0.5, 0.75),
    }


def dilated(field, kernel, spread):
    result = lax.conv_general_dilated(field[None], kernel, (1, 1), ((spread, spread), (spread, spread)), rhs_dilation=(spread, spread), dimension_numbers=("NHWC", "HWIO", "NHWC"), preferred_element_type=jnp.float32)
    return result[0]


def reference(contact_map, first_kernel, second_kernel, project_weight):
    first = jnp.maximum(dilated(contact_map, first_kernel, 4), 0.0).astype(jnp.bfloat16)
    mirror = jnp.transpose(first, (1, 0, 2))
    sym = (0.5 * (first.astype(jnp.float32) + mirror.astype(jnp.float32))).astype(jnp.bfloat16)
    second = jnp.maximum(dilated(sym, second_kernel, 8), 0.0).astype(jnp.bfloat16)
    side = lax.dot_general(second, project_weight, (((2,), (0,)), ((), ())), preferred_element_type=jnp.float32)
    return (contact_map.astype(jnp.float32) + side).astype(jnp.bfloat16)
```

```python
import functools

import jax
import jax.numpy as jnp
from jax import lax
from jax.experimental import pallas as pl
from jax.experimental.pallas import tpu as pltpu
from jax.sharding import PartitionSpec as P

NEAR = 4
FAR = 8
BF16 = jnp.bfloat16
F32 = jnp.float32


def loop(count, body):
    if count == 1:
        body(0)
    else:
        lax.fori_loop(0, count, lambda i, c: (body(i), c)[1], 0)


def block_kernel(
    n, pieces, x_hbm, k1_hbm, k2_hbm, pw_hbm, out_ref,
    xpad, w1, w2, wp, first, turned, mirror, sym3, acc,
    load_sem, halo_send, halo_recv, turn_send, turn_recv, edge_send, edge_recv,
):
    rows, width, chans = x_hbm.shape
    tile = rows * FAR
    blocks = width // FAR
    me = lax.axis_index("row")
    up, down = me - 1, me + 1
    has_up, has_down = me > 0, me < n - 1

    loads = [
        pltpu.make_async_copy(x_hbm, xpad.at[pl.ds(NEAR, rows)], load_sem.at[0]),
        pltpu.make_async_copy(k1_hbm, w1, load_sem.at[1]),
        pltpu.make_async_copy(k2_hbm, w2, load_sem.at[2]),
        pltpu.make_async_copy(pw_hbm, wp, load_sem.at[3]),
    ]
    for load in loads:
        load.start()

    barrier = pltpu.get_barrier_semaphore()

    def greet(k):
        pl.semaphore_signal(
            barrier, inc=1, device_id={"row": lax.rem(me + k + 1, n)},
            device_id_type=pl.DeviceIdType.MESH,
        )

    loop(n - 1, greet)

    zeros = jnp.zeros((tile, chans), BF16)
    for strip in range(3):
        sym3[strip, 0] = zeros
        sym3[strip, blocks + 1] = zeros

    @pl.when(jnp.logical_not(has_up))
    def _():
        xpad[0:NEAR] = jnp.zeros((NEAR, width, chans), BF16)

        def clear(s):
            sym3[0, s + 1] = zeros

        loop(blocks, clear)

    @pl.when(jnp.logical_not(has_down))
    def _():
        xpad[NEAR + rows :] = jnp.zeros((NEAR, width, chans), BF16)

        def clear(s):
            sym3[2, s + 1] = zeros

        loop(blocks, clear)

    def remote(src, dst, send, recv, target):
        return pltpu.make_async_remote_copy(
            src_ref=src, dst_ref=dst, send_sem=send, recv_sem=recv,
            device_id={"row": target}, device_id_type=pl.DeviceIdType.MESH,
        )

    to_up = remote(
        x_hbm.at[pl.ds(0, NEAR)], xpad.at[pl.ds(NEAR + rows, NEAR)],
        halo_send.at[0], halo_recv.at[0], up,
    )
    to_down = remote(
        x_hbm.at[pl.ds(rows - NEAR, NEAR)], xpad.at[pl.ds(0, NEAR)],
        halo_send.at[1], halo_recv.at[1], down,
    )

    pl.semaphore_wait(barrier, n - 1)

    @pl.when(has_up)
    def _():
        to_up.start()

    @pl.when(has_down)
    def _():
        to_down.start()

    loads[0].wait()
    loads[1].wait()

    step = max(1, min(NEAR, 512 // width))
    depth = step * width
    column = lax.rem(lax.broadcasted_iota(jnp.int32, (depth, chans), 0), width)

    def taps(parts, kinds):
        lhs = jnp.concatenate(parts, axis=1) if len(parts) > 1 else parts[0]
        rhs = [jnp.concatenate([w1[k, d] for d in range(3)], axis=1) for k in kinds]
        rhs = jnp.concatenate(rhs, axis=0) if len(rhs) > 1 else rhs[0]
        prod = jnp.dot(lhs, rhs, preferred_element_type=F32)
        left = pltpu.roll(prod[:, :chans], NEAR, 0)
        right = pltpu.roll(prod[:, 2 * chans :], depth - NEAR, 0)
        return (
            prod[:, chans : 2 * chans]
            + jnp.where(column >= NEAR, left, 0.0)
            + jnp.where(column < width - NEAR, right, 0.0)
        )

    def strip_of(row):
        return xpad[pl.ds(row, step)].reshape(depth, chans)

    def span(row):
        return pl.ds(pl.multiple_of(row * width, depth), depth)

    def inner(g):
        a = g * step
        near, mid = strip_of(NEAR + a), strip_of(2 * NEAR + a)
        first[span(a)] = taps([near, mid], (1, 2))
        first[span(NEAR + a)] = taps([near, mid], (0, 1))

    loop(NEAR // step, inner)

    @pl.when(has_up)
    def _():
        to_down.wait_recv()

    @pl.when(has_down)
    def _():
        to_up.wait_recv()

    def outer(g):
        a = g * step
        for row, source, kind in ((a, a, 0), (NEAR + a, rows + NEAR + a, 2)):
            total = first[span(row)] + taps([strip_of(source)], (kind,))
            first[span(row)] = jnp.maximum(total, 0.0).astype(BF16).astype(F32)

    loop(NEAR // step, outer)

    def turn(s):
        base = pl.multiple_of(s * FAR, FAR)
        cols = [first[pl.ds(base + j, rows, stride=width), :] for j in range(FAR)]
        return jnp.concatenate(cols, axis=0).astype(BF16)

    def turn_copy(s, k):
        return remote(turned.at[s], mirror.at[me], turn_send.at[k], turn_recv.at[me], s)

    def send_turn(t):
        k = 1 + lax.rem(t + n // 2 - 1, n - 1)
        s = lax.rem(me + k, n)
        turned[s] = turn(s)
        turn_copy(s, k).start()

    loop(n - 1, send_turn)
    mirror[me] = turn(me)

    per = n // pieces
    mine = me // per

    def edge_copies(p):
        part = pl.ds(1 + p * per, per)
        return (
            remote(sym3.at[1, part], sym3.at[2, part], edge_send.at[0, p], edge_recv.at[0, p], up),
            remote(sym3.at[1, part], sym3.at[0, part], edge_send.at[1, p], edge_recv.at[1, p], down),
        )

    def make_piece(q):
        p = lax.rem(mine + q, pieces)

        def make(b):
            s = p * per + b

            @pl.when(s != me)
            def _():
                remote(
                    turned.at[s], mirror.at[s], turn_send.at[0], turn_recv.at[s], s
                ).wait_recv()

            base = pl.multiple_of(s * FAR, FAR)
            own = [first[pl.ds(pl.multiple_of(base + i * width, FAR), FAR), :] for i in range(rows)]
            own = jnp.concatenate(own, axis=0)
            sym3[1, s + 1] = (0.5 * (own + mirror[s].astype(F32))).astype(BF16)

        loop(per, make)
        to_above, to_below = edge_copies(p)

        @pl.when(has_up)
        def _():
            to_above.start()

        @pl.when(has_down)
        def _():
            to_below.start()

    loop(pieces, make_piece)

    loads[2].wait()
    loads[3].wait()
    group = min(blocks, 16)
    high = group * tile

    def rows_of(strip, start):
        return sym3[strip, pl.ds(start, group)].reshape(high, chans)

    def product(strips, start):
        lhs = [rows_of(k, start + d) for k in strips for d in range(3)]
        rhs = [w2[k, d] for k in strips for d in range(3)]
        return jnp.dot(
            jnp.concatenate(lhs, axis=1), jnp.concatenate(rhs, axis=0),
            preferred_element_type=F32,
        )

    def middle(g):
        acc[pl.ds(pl.multiple_of(g * high, high), high)] = product((1,), g * group)

    loop(blocks // group, middle)

    def wait_edge(p):
        to_above, to_below = edge_copies(p)

        @pl.when(has_down)
        def _():
            to_above.wait_recv()

        @pl.when(has_up)
        def _():
            to_below.wait_recv()

    loop(pieces, wait_edge)

    def finish(g):
        total = acc[pl.ds(pl.multiple_of(g * high, high), high)] + product((0, 2), g * group)
        second = jnp.maximum(total, 0.0).astype(BF16)
        side = jnp.dot(second, wp[...], preferred_element_type=F32)
        side = side.reshape(group, rows, FAR, chans)
        part = pl.ds(pl.multiple_of(g * group * FAR, group * FAR), group * FAR)
        for i in range(rows):
            base = xpad[NEAR + i, part].astype(F32)
            out_ref[i, part] = (base + side[:, i].reshape(group * FAR, chans)).astype(BF16)

    loop(blocks // group, finish)

    @pl.when(has_up)
    def _():
        to_up.wait_send()

    @pl.when(has_down)
    def _():
        to_down.wait_send()

    def drain(t):
        turn_copy(lax.rem(me + t + 1, n), t + 1).wait_send()

    loop(n - 1, drain)

    def drain_edge(p):
        to_above, to_below = edge_copies(p)

        @pl.when(has_up)
        def _():
            to_above.wait_send()

        @pl.when(has_down)
        def _():
            to_below.wait_send()

    loop(pieces, drain_edge)


def shards(contact_map, first_kernel, second_kernel, project_weight):
    rows, width, chans = contact_map.shape
    n = lax.axis_size("row")
    assert rows == FAR and rows == 2 * NEAR and width == n * rows
    tile = rows * FAR
    blocks = width // FAR
    pieces = 4 if n % 4 == 0 else 1
    moved = 9 * chans * chans * 4 + 4 * rows * width * chans
    return pl.pallas_call(
        functools.partial(block_kernel, n, pieces),
        out_shape=jax.ShapeDtypeStruct(contact_map.shape, BF16),
        in_specs=[pl.BlockSpec(memory_space=pl.ANY)] * 4,
        out_specs=pl.BlockSpec(memory_space=pltpu.VMEM),
        scratch_shapes=[
            pltpu.VMEM((rows + 2 * NEAR, width, chans), BF16),
            pltpu.VMEM(first_kernel.shape, BF16),
            pltpu.VMEM(second_kernel.shape, BF16),
            pltpu.VMEM(project_weight.shape, BF16),
            pltpu.VMEM((rows * width, chans), F32),
            pltpu.VMEM((n, tile, chans), BF16),
            pltpu.VMEM((n, tile, chans), BF16),
            pltpu.VMEM((3, blocks + 2, tile, chans), BF16),
            pltpu.VMEM((rows * width, chans), F32),
            pltpu.SemaphoreType.DMA((4,)),
            pltpu.SemaphoreType.DMA((2,)),
            pltpu.SemaphoreType.DMA((2,)),
            pltpu.SemaphoreType.DMA((n,)),
            pltpu.SemaphoreType.DMA((n,)),
            pltpu.SemaphoreType.DMA((2, pieces)),
            pltpu.SemaphoreType.DMA((2, pieces)),
        ],
        compiler_params=pltpu.CompilerParams(
            collective_id=0, has_side_effects=True, vmem_limit_bytes=48 * 1024 * 1024
        ),
        cost_estimate=pl.CostEstimate(
            flops=2 * 19 * rows * width * chans * chans, bytes_accessed=moved, transcendentals=0
        ),
    )(contact_map, first_kernel, second_kernel, project_weight)


def solution(mesh):
    placed = (P(("win", "row"), None, None), P(), P(), P())
    return jax.shard_map(
        shards, mesh=mesh, in_specs=placed, out_specs=P(("win", "row"), None, None), check_vma=False
    )
```

```python
import functools

import jax
import jax.numpy as jnp
from jax import lax
from jax.experimental import pallas as pl
from jax.experimental.pallas import tpu as pltpu
from jax.sharding import PartitionSpec as P

NEAR = 4
FAR = 8
BF16 = jnp.bfloat16
F32 = jnp.float32


def loop(count, body):
    if count == 1:
        body(0)
    else:
        lax.fori_loop(0, count, lambda i, c: (body(i), c)[1], 0)


def block_kernel(
    n, pieces, x_hbm, k1_hbm, k2_hbm, pw_hbm, out_ref,
    xpad, w1, w2, wp, first, turned, mirror, sym3, acc,
    load_sem, halo_send, halo_recv, turn_send, turn_recv, edge_send, edge_recv,
):
    rows, width, chans = x_hbm.shape
    tile = rows * FAR
    blocks = width // FAR
    me = lax.axis_index("row")
    up, down = me - 1, me + 1
    has_up, has_down = me > 0, me < n - 1

    loads = [
        pltpu.make_async_copy(x_hbm, xpad.at[pl.ds(NEAR, rows)], load_sem.at[0]),
        pltpu.make_async_copy(k1_hbm, w1, load_sem.at[1]),
        pltpu.make_async_copy(k2_hbm, w2, load_sem.at[2]),
        pltpu.make_async_copy(pw_hbm, wp, load_sem.at[3]),
    ]
    for load in loads:
        load.start()

    barrier = pltpu.get_barrier_semaphore()

    def greet(k):
        pl.semaphore_signal(
            barrier, inc=1, device_id={"row": lax.rem(me + k + 1, n)},
            device_id_type=pl.DeviceIdType.MESH,
        )

    loop(n - 1, greet)

    zeros = jnp.zeros((tile, chans), BF16)
    for strip in range(3):
        sym3[strip, 0] = zeros
        sym3[strip, blocks + 1] = zeros

    @pl.when(jnp.logical_not(has_up))
    def _():
        xpad[0:NEAR] = jnp.zeros((NEAR, width, chans), BF16)

        def clear(s):
            sym3[0, s + 1] = zeros

        loop(blocks, clear)

    @pl.when(jnp.logical_not(has_down))
    def _():
        xpad[NEAR + rows :] = jnp.zeros((NEAR, width, chans), BF16)

        def clear(s):
            sym3[2, s + 1] = zeros

        loop(blocks, clear)

    def remote(src, dst, send, recv, target):
        return pltpu.make_async_remote_copy(
            src_ref=src, dst_ref=dst, send_sem=send, recv_sem=recv,
            device_id={"row": target}, device_id_type=pl.DeviceIdType.MESH,
        )

    to_up = remote(
        x_hbm.at[pl.ds(0, NEAR)], xpad.at[pl.ds(NEAR + rows, NEAR)],
        halo_send.at[0], halo_recv.at[0], up,
    )
    to_down = remote(
        x_hbm.at[pl.ds(rows - NEAR, NEAR)], xpad.at[pl.ds(0, NEAR)],
        halo_send.at[1], halo_recv.at[1], down,
    )

    pl.semaphore_wait(barrier, n - 1)

    @pl.when(has_up)
    def _():
        to_up.start()

    @pl.when(has_down)
    def _():
        to_down.start()

    loads[0].wait()
    loads[1].wait()

    step = max(1, min(NEAR, 512 // width))
    depth = step * width
    column = lax.rem(lax.broadcasted_iota(jnp.int32, (depth, chans), 0), width)

    def taps(parts, kinds):
        lhs = jnp.concatenate(parts, axis=1) if len(parts) > 1 else parts[0]
        rhs = [jnp.concatenate([w1[k, d] for d in range(3)], axis=1) for k in kinds]
        rhs = jnp.concatenate(rhs, axis=0) if len(rhs) > 1 else rhs[0]
        prod = jnp.dot(lhs, rhs, preferred_element_type=F32)
        left = pltpu.roll(prod[:, :chans], NEAR, 0)
        right = pltpu.roll(prod[:, 2 * chans :], depth - NEAR, 0)
        return (
            prod[:, chans : 2 * chans]
            + jnp.where(column >= NEAR, left, 0.0)
            + jnp.where(column < width - NEAR, right, 0.0)
        )

    def strip_of(row):
        return xpad[pl.ds(row, step)].reshape(depth, chans)

    def span(row):
        return pl.ds(pl.multiple_of(row * width, depth), depth)

    def inner(g):
        a = g * step
        near, mid = strip_of(NEAR + a), strip_of(2 * NEAR + a)
        first[span(a)] = taps([near, mid], (1, 2))
        first[span(NEAR + a)] = taps([near, mid], (0, 1))

    loop(NEAR // step, inner)

    @pl.when(has_up)
    def _():
        to_down.wait_recv()

    @pl.when(has_down)
    def _():
        to_up.wait_recv()

    def outer(g):
        a = g * step
        for row, source, kind in ((a, a, 0), (NEAR + a, rows + NEAR + a, 2)):
            total = first[span(row)] + taps([strip_of(source)], (kind,))
            first[span(row)] = jnp.maximum(total, 0.0).astype(BF16).astype(F32)

    loop(NEAR // step, outer)

    def turn(s):
        base = pl.multiple_of(s * FAR, FAR)
        cols = [first[pl.ds(base + j, rows, stride=width), :] for j in range(FAR)]
        return jnp.concatenate(cols, axis=0).astype(BF16)

    def turn_copy(s, k):
        return remote(turned.at[s], mirror.at[me], turn_send.at[k], turn_recv.at[me], s)

    def send_turn(t):
        k = 1 + lax.rem(t + n // 2 - 1, n - 1)
        s = lax.rem(me + k, n)
        turned[s] = turn(s)
        turn_copy(s, k).start()

    loop(n - 1, send_turn)
    mirror[me] = turn(me)

    per = n // pieces
    mine = me // per

    def edge_copies(p):
        part = pl.ds(1 + p * per, per)
        return (
            remote(sym3.at[1, part], sym3.at[2, part], edge_send.at[0, p], edge_recv.at[0, p], up),
            remote(sym3.at[1, part], sym3.at[0, part], edge_send.at[1, p], edge_recv.at[1, p], down),
        )

    def make_piece(q):
        p = lax.rem(mine + q, pieces)

        def make(b):
            s = p * per + b

            @pl.when(s != me)
            def _():
                remote(
                    turned.at[s], mirror.at[s], turn_send.at[0], turn_recv.at[s], s
                ).wait_recv()

            base = pl.multiple_of(s * FAR, FAR)
            own = [first[pl.ds(pl.multiple_of(base + i * width, FAR), FAR), :] for i in range(rows)]
            own = jnp.concatenate(own, axis=0)
            sym3[1, s + 1] = (0.5 * (own + mirror[s].astype(F32))).astype(BF16)

        loop(per, make)
        to_above, to_below = edge_copies(p)

        @pl.when(has_up)
        def _():
            to_above.start()

        @pl.when(has_down)
        def _():
            to_below.start()

    loop(pieces, make_piece)

    loads[2].wait()
    loads[3].wait()
    group = min(blocks, 16)
    high = group * tile

    def rows_of(strip, start):
        return sym3[strip, pl.ds(start, group)].reshape(high, chans)

    def product(strips, start):
        lhs = [rows_of(k, start + d) for k in strips for d in range(3)]
        rhs = [w2[k, d] for k in strips for d in range(3)]
        return jnp.dot(
            jnp.concatenate(lhs, axis=1), jnp.concatenate(rhs, axis=0),
            preferred_element_type=F32,
        )

    def middle(g):
        acc[pl.ds(pl.multiple_of(g * high, high), high)] = product((1,), g * group)

    loop(blocks // group, middle)

    def wait_edge(p):
        to_above, to_below = edge_copies(p)

        @pl.when(has_down)
        def _():
            to_above.wait_recv()

        @pl.when(has_up)
        def _():
            to_below.wait_recv()

    loop(pieces, wait_edge)

    def finish(g):
        total = acc[pl.ds(pl.multiple_of(g * high, high), high)] + product((0, 2), g * group)
        second = jnp.maximum(total, 0.0).astype(BF16)
        side = jnp.dot(second, wp[...], preferred_element_type=F32)
        side = side.reshape(group, rows, FAR, chans)
        part = pl.ds(pl.multiple_of(g * group * FAR, group * FAR), group * FAR)
        for i in range(rows):
            base = xpad[NEAR + i, part].astype(F32)
            out_ref[i, part] = (base + side[:, i].reshape(group * FAR, chans)).astype(BF16)

    loop(blocks // group, finish)

    @pl.when(has_up)
    def _():
        to_up.wait_send()

    @pl.when(has_down)
    def _():
        to_down.wait_send()

    def drain(t):
        turn_copy(lax.rem(me + t + 1, n), t + 1).wait_send()

    loop(n - 1, drain)

    def drain_edge(p):
        to_above, to_below = edge_copies(p)

        @pl.when(has_up)
        def _():
            to_above.wait_send()

        @pl.when(has_down)
        def _():
            to_below.wait_send()

    loop(pieces, drain_edge)


def shards(contact_map, first_kernel, second_kernel, project_weight):
    rows, width, chans = contact_map.shape
    n = lax.axis_size("row")
    assert rows == FAR and rows == 2 * NEAR and width == n * rows
    tile = rows * FAR
    blocks = width // FAR
    pieces = 4 if n % 4 == 0 else 1
    moved = 9 * chans * chans * 4 + 4 * rows * width * chans
    return pl.pallas_call(
        functools.partial(block_kernel, n, pieces),
        out_shape=jax.ShapeDtypeStruct(contact_map.shape, BF16),
        in_specs=[pl.BlockSpec(memory_space=pltpu.HBM)] * 4,
        out_specs=pl.BlockSpec(memory_space=pltpu.VMEM),
        scratch_shapes=[
            pltpu.VMEM((rows + 2 * NEAR, width, chans), BF16),
            pltpu.VMEM(first_kernel.shape, BF16),
            pltpu.VMEM(second_kernel.shape, BF16),
            pltpu.VMEM(project_weight.shape, BF16),
            pltpu.VMEM((rows * width, chans), F32),
            pltpu.VMEM((n, tile, chans), BF16),
            pltpu.VMEM((n, tile, chans), BF16),
            pltpu.VMEM((3, blocks + 2, tile, chans), BF16),
            pltpu.VMEM((rows * width, chans), F32),
            pltpu.SemaphoreType.DMA((4,)),
            pltpu.SemaphoreType.DMA((2,)),
            pltpu.SemaphoreType.DMA((2,)),
            pltpu.SemaphoreType.DMA((n,)),
            pltpu.SemaphoreType.DMA((n,)),
            pltpu.SemaphoreType.DMA((2, pieces)),
            pltpu.SemaphoreType.DMA((2, pieces)),
        ],
        compiler_params=pltpu.CompilerParams(
            collective_id=0, has_side_effects=True, vmem_limit_bytes=48 * 1024 * 1024
        ),
        cost_estimate=pl.CostEstimate(
            flops=2 * 19 * rows * width * chans * chans, bytes_accessed=moved, transcendentals=0
        ),
    )(contact_map, first_kernel, second_kernel, project_weight)


def solution(mesh):
    placed = (P(("win", "row"), None, None), P(), P(), P())
    return jax.shard_map(
        shards, mesh=mesh, in_specs=placed, out_specs=P(("win", "row"), None, None), check_vma=False
    )
```

```python
import functools

import jax
import jax.numpy as jnp
from jax import lax
from jax.experimental import pallas as pl
from jax.experimental.pallas import tpu as pltpu
from jax.sharding import PartitionSpec as P

NEAR = 4
FAR = 8
BF16 = jnp.bfloat16
F32 = jnp.float32


def loop(count, body):
    if count == 1:
        body(0)
    else:
        lax.fori_loop(0, count, lambda i, c: (body(i), c)[1], 0)


def block_kernel(
    n, x_hbm, k1_hbm, k2_hbm, pw_hbm, out_ref,
    xpad, w1, w2, wp, first, turned, mirror, sym3, acc,
    load_sem, halo_send, halo_recv, turn_send, turn_recv, edge_send, edge_recv,
):
    rows, width, chans = x_hbm.shape
    tile = rows * FAR
    blocks = width // FAR
    me = lax.axis_index("row")
    up, down = me - 1, me + 1
    has_up, has_down = me > 0, me < n - 1

    loads = [
        pltpu.make_async_copy(x_hbm, xpad.at[pl.ds(NEAR, rows)], load_sem.at[0]),
        pltpu.make_async_copy(k1_hbm, w1, load_sem.at[1]),
        pltpu.make_async_copy(k2_hbm, w2, load_sem.at[2]),
        pltpu.make_async_copy(pw_hbm, wp, load_sem.at[3]),
    ]
    for load in loads:
        load.start()

    barrier = pltpu.get_barrier_semaphore()

    def greet(k):
        pl.semaphore_signal(
            barrier, inc=1, device_id={"row": lax.rem(me + k + 1, n)},
            device_id_type=pl.DeviceIdType.MESH,
        )

    loop(n - 1, greet)

    zeros = jnp.zeros((tile, chans), BF16)
    for strip in range(3):
        sym3[strip, 0] = zeros
        sym3[strip, blocks + 1] = zeros

    @pl.when(jnp.logical_not(has_up))
    def _():
        xpad[0:NEAR] = jnp.zeros((NEAR, width, chans), BF16)

        def clear(s):
            sym3[0, s + 1] = zeros

        loop(blocks, clear)

    @pl.when(jnp.logical_not(has_down))
    def _():
        xpad[NEAR + rows :] = jnp.zeros((NEAR, width, chans), BF16)

        def clear(s):
            sym3[2, s + 1] = zeros

        loop(blocks, clear)

    def remote(src, dst, send, recv, target):
        return pltpu.make_async_remote_copy(
            src_ref=src, dst_ref=dst, send_sem=send, recv_sem=recv,
            device_id={"row": target}, device_id_type=pl.DeviceIdType.MESH,
        )

    to_up = remote(
        x_hbm.at[pl.ds(0, NEAR)], xpad.at[pl.ds(NEAR + rows, NEAR)],
        halo_send.at[0], halo_recv.at[0], up,
    )
    to_down = remote(
        x_hbm.at[pl.ds(rows - NEAR, NEAR)], xpad.at[pl.ds(0, NEAR)],
        halo_send.at[1], halo_recv.at[1], down,
    )

    pl.semaphore_wait(barrier, n - 1)

    pl.when(has_up)(to_up.start)
    pl.when(has_down)(to_down.start)

    loads[0].wait()
    loads[1].wait()

    step = max(1, min(NEAR, 512 // width))
    depth = step * width
    column = lax.rem(lax.broadcasted_iota(jnp.int32, (depth, chans), 0), width)

    def taps(parts, kinds):
        lhs = jnp.concatenate(parts, axis=1) if len(parts) > 1 else parts[0]
        rhs = [jnp.concatenate([w1[k, d] for d in range(3)], axis=1) for k in kinds]
        rhs = jnp.concatenate(rhs, axis=0) if len(rhs) > 1 else rhs[0]
        prod = jnp.dot(lhs, rhs, preferred_element_type=F32)
        left = pltpu.roll(prod[:, :chans], NEAR, 0)
        right = pltpu.roll(prod[:, 2 * chans :], depth - NEAR, 0)
        return (
            prod[:, chans : 2 * chans]
            + jnp.where(column >= NEAR, left, 0.0)
            + jnp.where(column < width - NEAR, right, 0.0)
        )

    def strip_of(row):
        return xpad[pl.ds(row, step)].reshape(depth, chans)

    def span(row):
        return pl.ds(pl.multiple_of(row * width, depth), depth)

    def inner(g):
        a = g * step
        near, mid = strip_of(NEAR + a), strip_of(2 * NEAR + a)
        first[span(a)] = taps([near, mid], (1, 2))
        first[span(NEAR + a)] = taps([near, mid], (0, 1))

    loop(NEAR // step, inner)

    pl.when(has_up)(to_down.wait_recv)
    pl.when(has_down)(to_up.wait_recv)

    def outer(g):
        a = g * step
        for row, source, kind in ((a, a, 0), (NEAR + a, rows + NEAR + a, 2)):
            total = first[span(row)] + taps([strip_of(source)], (kind,))
            first[span(row)] = jnp.maximum(total, 0.0).astype(BF16).astype(F32)

    loop(NEAR // step, outer)

    def turn(s):
        base = pl.multiple_of(s * FAR, FAR)
        cols = [first[pl.ds(base + j, rows, stride=width), :] for j in range(FAR)]
        return jnp.concatenate(cols, axis=0).astype(BF16)

    def turn_copy(s):
        return remote(turned.at[s], mirror.at[me], turn_send.at[s], turn_recv.at[me], s)

    def at_distance(d, visit):
        for s, there in ((me - d, me >= d), (me + d, me + d < n)):
            pl.when(there)(functools.partial(visit, s))

    def send_turn(t):
        def visit(s):
            turned[s] = turn(s)
            turn_copy(s).start()

        at_distance(n - 1 - t, visit)

    loop(n - 1, send_turn)

    def edge_copies(s):
        block = sym3.at[1, s + 1]
        return (
            remote(block, sym3.at[2, s + 1], edge_send.at[0, s], edge_recv.at[0, s], up),
            remote(block, sym3.at[0, s + 1], edge_send.at[1, s], edge_recv.at[1, s], down),
        )

    def make_block(s, other):
        base = pl.multiple_of(s * FAR, FAR)
        own = [first[pl.ds(pl.multiple_of(base + i * width, FAR), FAR), :] for i in range(rows)]
        own = jnp.concatenate(own, axis=0)
        sym3[1, s + 1] = (0.5 * (own + other.astype(F32))).astype(BF16)
        to_above, to_below = edge_copies(s)
        pl.when(has_up)(to_above.start)
        pl.when(has_down)(to_below.start)

    make_block(me, turn(me))

    def take_turn(t):
        def visit(s):
            remote(
                turned.at[s], mirror.at[s], turn_send.at[s], turn_recv.at[s], s
            ).wait_recv()
            make_block(s, mirror[s])

        at_distance(t + 1, visit)

    loop(n - 1, take_turn)

    loads[2].wait()
    loads[3].wait()
    group = min(blocks, 16)
    high = group * tile

    def rows_of(strip, start):
        return sym3[strip, pl.ds(start, group)].reshape(high, chans)

    def product(strips, start):
        lhs = [rows_of(k, start + d) for k in strips for d in range(3)]
        rhs = [w2[k, d] for k in strips for d in range(3)]
        return jnp.dot(
            jnp.concatenate(lhs, axis=1), jnp.concatenate(rhs, axis=0),
            preferred_element_type=F32,
        )

    def middle(g):
        acc[pl.ds(pl.multiple_of(g * high, high), high)] = product((1,), g * group)

    loop(blocks // group, middle)

    def wait_edge(s):
        to_above, to_below = edge_copies(s)
        pl.when(has_down)(to_above.wait_recv)
        pl.when(has_up)(to_below.wait_recv)

    loop(n, wait_edge)

    def finish(g):
        total = acc[pl.ds(pl.multiple_of(g * high, high), high)] + product((0, 2), g * group)
        second = jnp.maximum(total, 0.0).astype(BF16)
        side = jnp.dot(second, wp[...], preferred_element_type=F32)
        side = side.reshape(group, rows, FAR, chans)
        part = pl.ds(pl.multiple_of(g * group * FAR, group * FAR), group * FAR)
        for i in range(rows):
            base = xpad[NEAR + i, part].astype(F32)
            out_ref[i, part] = (base + side[:, i].reshape(group * FAR, chans)).astype(BF16)

    loop(blocks // group, finish)

    pl.when(has_up)(to_up.wait_send)
    pl.when(has_down)(to_down.wait_send)

    def drain(s):
        @pl.when(s != me)
        def _():
            turn_copy(s).wait_send()

        to_above, to_below = edge_copies(s)
        pl.when(has_up)(to_above.wait_send)
        pl.when(has_down)(to_below.wait_send)

    loop(n, drain)


def shards(contact_map, first_kernel, second_kernel, project_weight):
    rows, width, chans = contact_map.shape
    n = lax.axis_size("row")
    assert rows == FAR and rows == 2 * NEAR and width == n * rows
    tile = rows * FAR
    blocks = width // FAR
    moved = 9 * chans * chans * 4 + 4 * rows * width * chans
    return pl.pallas_call(
        functools.partial(block_kernel, n),
        out_shape=jax.ShapeDtypeStruct(contact_map.shape, BF16),
        in_specs=[pl.BlockSpec(memory_space=pltpu.HBM)] * 4,
        out_specs=pl.BlockSpec(memory_space=pltpu.VMEM),
        scratch_shapes=[
            pltpu.VMEM((rows + 2 * NEAR, width, chans), BF16),
            pltpu.VMEM(first_kernel.shape, BF16),
            pltpu.VMEM(second_kernel.shape, BF16),
            pltpu.VMEM(project_weight.shape, BF16),
            pltpu.VMEM((rows * width, chans), F32),
            pltpu.VMEM((n, tile, chans), BF16),
            pltpu.VMEM((n, tile, chans), BF16),
            pltpu.VMEM((3, blocks + 2, tile, chans), BF16),
            pltpu.VMEM((rows * width, chans), F32),
            pltpu.SemaphoreType.DMA((4,)),
            pltpu.SemaphoreType.DMA((2,)),
            pltpu.SemaphoreType.DMA((2,)),
            pltpu.SemaphoreType.DMA((n,)),
            pltpu.SemaphoreType.DMA((n,)),
            pltpu.SemaphoreType.DMA((2, n)),
            pltpu.SemaphoreType.DMA((2, n)),
        ],
        compiler_params=pltpu.CompilerParams(
            collective_id=0, has_side_effects=True, vmem_limit_bytes=64 * 1024 * 1024
        ),
        cost_estimate=pl.CostEstimate(
            flops=2 * 19 * rows * width * chans * chans, bytes_accessed=moved, transcendentals=0
        ),
    )(contact_map, first_kernel, second_kernel, project_weight)


def solution(mesh):
    placed = (P(("win", "row"), None, None), P(), P(), P())
    return jax.shard_map(
        shards, mesh=mesh, in_specs=placed, out_specs=P(("win", "row"), None, None), check_vma=False
    )
```

```python
import functools

import jax
import jax.numpy as jnp
from jax import lax
from jax.experimental import pallas as pl
from jax.experimental.pallas import tpu as pltpu
from jax.sharding import PartitionSpec as P

NEAR = 4
FAR = 8
REACH = 16
BF16 = jnp.bfloat16
F32 = jnp.float32


def loop(count, body):
    if count == 1:
        body(0)
    else:
        lax.fori_loop(0, count, lambda i, c: (body(i), c)[1], 0)


def block_kernel(
    n, x_hbm, k1_hbm, k2_hbm, pw_hbm, out_ref,
    xpad, w1, w2, wp, first, turned, mirror, sym3, acc,
    load_sem, halo_send, halo_recv, turn_send, turn_recv, edge_send, edge_recv,
):
    rows, width, chans = x_hbm.shape
    tile = rows * FAR
    blocks = width // FAR
    me = lax.axis_index("row")
    up, down = me - 1, me + 1
    has_up, has_down = me > 0, me < n - 1

    loads = [
        pltpu.make_async_copy(x_hbm, xpad.at[pl.ds(NEAR, rows)], load_sem.at[0]),
        pltpu.make_async_copy(k1_hbm, w1, load_sem.at[1]),
        pltpu.make_async_copy(k2_hbm, w2, load_sem.at[2]),
        pltpu.make_async_copy(pw_hbm, wp, load_sem.at[3]),
    ]
    for load in loads:
        load.start()

    barrier = pltpu.get_barrier_semaphore()

    def greet(k):
        pl.semaphore_signal(
            barrier, inc=1, device_id={"row": lax.rem(me + k + 1, n)},
            device_id_type=pl.DeviceIdType.MESH,
        )

    loop(n - 1, greet)

    zeros = jnp.zeros((tile, chans), BF16)
    for strip in range(3):
        sym3[strip, 0] = zeros
        sym3[strip, blocks + 1] = zeros

    @pl.when(jnp.logical_not(has_up))
    def _():
        xpad[0:NEAR] = jnp.zeros((NEAR, width, chans), BF16)

        def clear(s):
            sym3[0, s + 1] = zeros

        loop(blocks, clear)

    @pl.when(jnp.logical_not(has_down))
    def _():
        xpad[NEAR + rows :] = jnp.zeros((NEAR, width, chans), BF16)

        def clear(s):
            sym3[2, s + 1] = zeros

        loop(blocks, clear)

    def remote(src, dst, send, recv, target):
        return pltpu.make_async_remote_copy(
            src_ref=src, dst_ref=dst, send_sem=send, recv_sem=recv,
            device_id={"row": target}, device_id_type=pl.DeviceIdType.MESH,
        )

    half = n // 2
    cut = width // 2 + REACH
    parts = (((0, cut), (cut, width - cut)), ((width - cut, cut), (0, width - cut)))

    def halo(side, m, which):
        start, size = parts[which][m]
        cols = pl.ds(start, size)
        if side == 0:
            src, dst, target = pl.ds(0, NEAR), pl.ds(NEAR + rows, NEAR), up
        else:
            src, dst, target = pl.ds(rows - NEAR, NEAR), pl.ds(0, NEAR), down
        return remote(
            x_hbm.at[src, cols], xpad.at[dst, cols],
            halo_send.at[side, m], halo_recv.at[side, m], target,
        )

    def each_halo(visit):
        for which in (0, 1):
            for side, there, target in ((0, has_up, up), (1, has_down, down)):
                wanted = (target >= half) if which == 0 else (target < half)

                @pl.when(jnp.logical_and(there, wanted))
                def _():
                    for m in (0, 1):
                        visit(halo(side, m, which))

    pl.semaphore_wait(barrier, n - 1)

    each_halo(lambda copy: copy.start())

    loads[0].wait()
    loads[1].wait()

    step = max(1, min(NEAR, 512 // width))

    def taps(strips, kinds, wide):
        depth = step * wide
        lhs = [strip.reshape(depth, chans) for strip in strips]
        lhs = jnp.concatenate(lhs, axis=1) if len(lhs) > 1 else lhs[0]
        rhs = [jnp.concatenate([w1[k, d] for d in range(3)], axis=1) for k in kinds]
        rhs = jnp.concatenate(rhs, axis=0) if len(rhs) > 1 else rhs[0]
        prod = jnp.dot(lhs, rhs, preferred_element_type=F32)
        column = lax.rem(lax.broadcasted_iota(jnp.int32, (depth, chans), 0), wide)
        left = pltpu.roll(prod[:, :chans], NEAR, 0)
        right = pltpu.roll(prod[:, 2 * chans :], depth - NEAR, 0)
        return (
            prod[:, chans : 2 * chans]
            + jnp.where(column >= NEAR, left, 0.0)
            + jnp.where(column < wide - NEAR, right, 0.0)
        )

    def inner(g):
        a = g * step
        near, mid = xpad[pl.ds(NEAR + a, step)], xpad[pl.ds(2 * NEAR + a, step)]
        high = step * width
        for row, kinds in ((a, (1, 2)), (NEAR + a, (0, 1))):
            first[pl.ds(pl.multiple_of(row * width, width), high)] = taps([near, mid], kinds, width)

    loop(NEAR // step, inner)

    def outer(which, g):
        a = g * step
        keep = width // 2
        start, off = (0, 0) if which == 0 else (width - cut, REACH)
        for row, source, kind in ((a, a, 0), (NEAR + a, rows + NEAR + a, 2)):
            extra = taps([xpad[pl.ds(source, step), pl.ds(start, cut)]], (kind,), cut)
            for i in range(step):
                span = pl.ds(pl.multiple_of((row + i) * width + which * keep, keep), keep)
                total = first[span] + extra[i * cut + off : i * cut + off + keep]
                first[span] = jnp.maximum(total, 0.0).astype(BF16).astype(F32)

    def turn(s):
        base = pl.multiple_of(s * FAR, FAR)
        cols = [first[pl.ds(base + j, rows, stride=width), :] for j in range(FAR)]
        return jnp.concatenate(cols, axis=0).astype(BF16)

    def first_half(m, which):
        pl.when(has_up)(halo(1, m, m ^ which).wait_recv)
        pl.when(has_down)(halo(0, m, m ^ which).wait_recv)
        loop(NEAR // step, functools.partial(outer, which))

        def send_turn(t):
            s = which * half + lax.rem(me + t, half)

            @pl.when(s != me)
            def _():
                turned[s] = turn(s)
                remote(turned.at[s], mirror.at[me], turn_send.at[0], turn_recv.at[me], s).start()

        loop(half, send_turn)

    @pl.when(me < half)
    def _():
        first_half(0, 1)
        first_half(1, 0)

    @pl.when(me >= half)
    def _():
        first_half(0, 0)
        first_half(1, 1)

    def edge_copies(at, count):
        block = sym3.at[1, pl.ds(at, count)]
        return (
            remote(
                block, sym3.at[2, pl.ds(at, count)], edge_send.at[0], edge_recv.at[0], up
            ),
            remote(
                block, sym3.at[0, pl.ds(at, count)], edge_send.at[1], edge_recv.at[1], down
            ),
        )

    def make_block(s, other):
        base = pl.multiple_of(s * FAR, FAR)
        own = [first[pl.ds(pl.multiple_of(base + i * width, FAR), FAR), :] for i in range(rows)]
        own = jnp.concatenate(own, axis=0)
        sym3[1, s + 1] = (0.5 * (own + other.astype(F32))).astype(BF16)
        to_above, to_below = edge_copies(s + 1, 1)
        pl.when(has_up)(to_above.start)
        pl.when(has_down)(to_below.start)

    make_block(me, turn(me))
    home = (me // half) * half

    def take_turn(t):
        group = jnp.where(t < half, home, half - home)
        s = group + lax.rem(me - t + n, half)

        @pl.when(s != me)
        def _():
            remote(
                turned.at[s], mirror.at[s], turn_send.at[0], turn_recv.at[s], s
            ).wait_recv()
            make_block(s, mirror[s])

    loop(n, take_turn)

    loads[2].wait()
    loads[3].wait()
    group = min(blocks, 16)
    high = group * tile

    def rows_of(strip, start):
        return sym3[strip, pl.ds(start, group)].reshape(high, chans)

    def product(strips, start):
        lhs = [rows_of(k, start + d) for k in strips for d in range(3)]
        rhs = [w2[k, d] for k in strips for d in range(3)]
        return jnp.dot(
            jnp.concatenate(lhs, axis=1), jnp.concatenate(rhs, axis=0),
            preferred_element_type=F32,
        )

    def middle(g):
        acc[pl.ds(pl.multiple_of(g * high, high), high)] = product((1,), g * group)

    loop(blocks // group, middle)
    to_above, to_below = edge_copies(1, n)

    def arrived(strip):
        if strip == 0:
            pl.when(has_up)(to_below.wait_recv)
        else:
            pl.when(has_down)(to_above.wait_recv)

    def finish(strip, g):
        total = acc[pl.ds(pl.multiple_of(g * high, high), high)] + product((strip,), g * group)
        second = jnp.maximum(total, 0.0).astype(BF16)
        side = jnp.dot(second, wp[...], preferred_element_type=F32)
        side = side.reshape(group, rows, FAR, chans)
        part = pl.ds(pl.multiple_of(g * group * FAR, group * FAR), group * FAR)
        for i in range(rows):
            base = xpad[NEAR + i, part].astype(F32)
            out_ref[i, part] = (base + side[:, i].reshape(group * FAR, chans)).astype(BF16)

    def last_strips(early, late):
        arrived(early)

        def add(g):
            span = pl.ds(pl.multiple_of(g * high, high), high)
            acc[span] = acc[span] + product((early,), g * group)

        loop(blocks // group, add)
        arrived(late)
        loop(blocks // group, functools.partial(finish, late))

    pl.when(me % 2 == 0)(lambda: last_strips(2, 0))
    pl.when(me % 2 == 1)(lambda: last_strips(0, 2))

    each_halo(lambda copy: copy.wait_send())
    some = pl.ds(0, n - 1)
    remote(
        turned.at[some], mirror.at[some], turn_send.at[0], turn_recv.at[0], lax.rem(me + 1, n)
    ).wait_send()
    pl.when(has_up)(to_above.wait_send)
    pl.when(has_down)(to_below.wait_send)


def shards(contact_map, first_kernel, second_kernel, project_weight):
    args = (contact_map, first_kernel, second_kernel, project_weight)
    rows, width, chans = contact_map.shape
    n = lax.axis_size("row")
    assert rows == FAR and rows == 2 * NEAR and width == n * rows
    tile = rows * FAR
    blocks = width // FAR
    moved = 9 * chans * chans * 4 + 4 * rows * width * chans
    return pl.pallas_call(
        functools.partial(block_kernel, n),
        out_shape=pltpu.VMEM(contact_map.shape, BF16),
        in_specs=[pl.BlockSpec(memory_space=pltpu.HBM)] * 4,
        out_specs=pl.BlockSpec(memory_space=pltpu.VMEM),
        scratch_shapes=[
            pltpu.VMEM((rows + 2 * NEAR, width, chans), BF16),
            pltpu.VMEM(first_kernel.shape, BF16),
            pltpu.VMEM(second_kernel.shape, BF16),
            pltpu.VMEM(project_weight.shape, BF16),
            pltpu.VMEM((rows * width, chans), F32),
            pltpu.VMEM((n, tile, chans), BF16),
            pltpu.VMEM((n, tile, chans), BF16),
            pltpu.VMEM((3, blocks + 2, tile, chans), BF16),
            pltpu.VMEM((rows * width, chans), F32),
            pltpu.SemaphoreType.DMA((4,)),
            pltpu.SemaphoreType.DMA((2, 2)),
            pltpu.SemaphoreType.DMA((2, 2)),
            pltpu.SemaphoreType.DMA((1,)),
            pltpu.SemaphoreType.DMA((n,)),
            pltpu.SemaphoreType.DMA((2,)),
            pltpu.SemaphoreType.DMA((2,)),
        ],
        compiler_params=pltpu.CompilerParams(
            collective_id=0, has_side_effects=True, vmem_limit_bytes=60 * 1024 * 1024
        ),
        cost_estimate=pl.CostEstimate(
            flops=2 * 19 * rows * width * chans * chans, bytes_accessed=moved, transcendentals=0
        ),
    )(*(pltpu.with_memory_space_constraint(x, pltpu.HBM) for x in args))


def solution(mesh):
    placed = (P(("win", "row"), None, None), P(), P(), P())
    return jax.shard_map(
        shards, mesh=mesh, in_specs=placed, out_specs=P(("win", "row"), None, None), check_vma=False
    )
```

```python
import functools

import jax
import jax.numpy as jnp
from jax import lax
from jax.experimental import pallas as pl
from jax.experimental.pallas import tpu as pltpu
from jax.sharding import PartitionSpec as P

NEAR = 4
FAR = 8
REACH = 16
BF16 = jnp.bfloat16
F32 = jnp.float32


def loop(count, body):
    if count == 1:
        body(0)
    else:
        lax.fori_loop(0, count, lambda i, c: (body(i), c)[1], 0)


def short(count, body):
    if count <= 4:
        for i in range(count):
            body(i)
    else:
        loop(count, body)


def block_kernel(
    n, x_hbm, k1_hbm, k2_hbm, pw_hbm, out_ref,
    xpad, w1, w2, wp, first, turned, mirror, sym3, acc,
    load_sem, halo_send, halo_recv, turn_send, turn_recv, edge_send, edge_recv,
):
    rows, width, chans = x_hbm.shape
    tile = rows * FAR
    blocks = width // FAR
    me = lax.axis_index("row")
    up, down = me - 1, me + 1
    has_up, has_down = me > 0, me < n - 1

    loads = [
        pltpu.make_async_copy(x_hbm, xpad.at[pl.ds(NEAR, rows)], load_sem.at[0]),
        pltpu.make_async_copy(k1_hbm, w1, load_sem.at[1]),
        pltpu.make_async_copy(k2_hbm, w2, load_sem.at[2]),
        pltpu.make_async_copy(pw_hbm, wp, load_sem.at[3]),
    ]
    for load in loads:
        load.start()

    barrier = pltpu.get_barrier_semaphore()

    def greet(k):
        pl.semaphore_signal(
            barrier, inc=1, device_id={"row": lax.rem(me + k + 1, n)},
            device_id_type=pl.DeviceIdType.MESH,
        )

    loop(n - 1, greet)

    zeros = jnp.zeros((tile, chans), BF16)
    for strip in range(3):
        sym3[strip, 0] = zeros
        sym3[strip, blocks + 1] = zeros

    @pl.when(jnp.logical_not(has_up))
    def _():
        xpad[0:NEAR] = jnp.zeros((NEAR, width, chans), BF16)

        def clear(s):
            sym3[0, s + 1] = zeros

        loop(blocks, clear)

    @pl.when(jnp.logical_not(has_down))
    def _():
        xpad[NEAR + rows :] = jnp.zeros((NEAR, width, chans), BF16)

        def clear(s):
            sym3[2, s + 1] = zeros

        loop(blocks, clear)

    def remote(src, dst, send, recv, target):
        return pltpu.make_async_remote_copy(
            src_ref=src, dst_ref=dst, send_sem=send, recv_sem=recv,
            device_id={"row": target}, device_id_type=pl.DeviceIdType.MESH,
        )

    half = n // 2
    cut = width // 2 + REACH
    parts = (((0, cut), (cut, width - cut)), ((width - cut, cut), (0, width - cut)))

    def halo(side, m, which):
        start, size = parts[which][m]
        cols = pl.ds(start, size)
        if side == 0:
            src, dst, target = pl.ds(0, NEAR), pl.ds(NEAR + rows, NEAR), up
        else:
            src, dst, target = pl.ds(rows - NEAR, NEAR), pl.ds(0, NEAR), down
        return remote(
            x_hbm.at[src, cols], xpad.at[dst, cols],
            halo_send.at[side, m], halo_recv.at[side, m], target,
        )

    def each_halo(visit):
        for which in (0, 1):
            for side, there, target in ((0, has_up, up), (1, has_down, down)):
                wanted = (target >= half) if which == 0 else (target < half)

                @pl.when(jnp.logical_and(there, wanted))
                def _():
                    for m in (0, 1):
                        visit(halo(side, m, which))

    pl.semaphore_wait(barrier, n - 1)

    each_halo(lambda copy: copy.start())

    loads[0].wait()
    loads[1].wait()

    step = max(1, min(NEAR, 512 // width))

    def taps(strips, kinds, wide):
        depth = step * wide
        lhs = [strip.reshape(depth, chans) for strip in strips]
        lhs = jnp.concatenate(lhs, axis=1) if len(lhs) > 1 else lhs[0]
        rhs = [jnp.concatenate([w1[k, d] for d in range(3)], axis=1) for k in kinds]
        rhs = jnp.concatenate(rhs, axis=0) if len(rhs) > 1 else rhs[0]
        prod = jnp.dot(lhs, rhs, preferred_element_type=F32)
        column = lax.broadcasted_iota(jnp.int32, (step, wide, chans), 1).reshape(depth, chans)
        left = pltpu.roll(prod[:, :chans], NEAR, 0)
        right = pltpu.roll(prod[:, 2 * chans :], depth - NEAR, 0)
        return (
            prod[:, chans : 2 * chans]
            + jnp.where(column >= NEAR, left, 0.0)
            + jnp.where(column < wide - NEAR, right, 0.0)
        )

    def inner(g):
        a = g * step
        near, mid = xpad[pl.ds(NEAR + a, step)], xpad[pl.ds(2 * NEAR + a, step)]
        high = step * width
        for row, kinds in ((a, (1, 2)), (NEAR + a, (0, 1))):
            first[pl.ds(pl.multiple_of(row * width, width), high)] = taps([near, mid], kinds, width)

    loop(NEAR // step, inner)

    def outer(which, g):
        a = g * step
        keep = width // 2
        start, off = (0, 0) if which == 0 else (width - cut, REACH)
        for row, source, kind in ((a, a, 0), (NEAR + a, rows + NEAR + a, 2)):
            extra = taps([xpad[pl.ds(source, step), pl.ds(start, cut)]], (kind,), cut)
            for i in range(step):
                span = pl.ds(pl.multiple_of((row + i) * width + which * keep, keep), keep)
                total = first[span] + extra[i * cut + off : i * cut + off + keep]
                first[span] = jnp.maximum(total, 0.0).astype(BF16).astype(F32)

    def turn(s):
        base = pl.multiple_of(s * FAR, FAR)
        cols = [first[pl.ds(base + j, rows, stride=width), :] for j in range(FAR)]
        return jnp.concatenate(cols, axis=0).astype(BF16)

    per = n // 4
    mine = me // per

    def first_half(m, which):
        pl.when(has_up)(halo(1, m, m ^ which).wait_recv)
        pl.when(has_down)(halo(0, m, m ^ which).wait_recv)
        loop(NEAR // step, functools.partial(outer, which))

        for far in ((2, 3) if m == 0 else (1, 0)):
            group = mine ^ far

            def send_turn(t):
                s = group * per + lax.rem(me + t, per)

                @pl.when(s != me)
                def _():
                    turned[s] = turn(s)
                    remote(
                        turned.at[s], mirror.at[me], turn_send.at[0], turn_recv.at[mine], s
                    ).start()

            short(per, send_turn)

    @pl.when(me < half)
    def _():
        first_half(0, 1)
        first_half(1, 0)

    @pl.when(me >= half)
    def _():
        first_half(0, 0)
        first_half(1, 1)

    def edge_copies(at, count):
        block = sym3.at[1, pl.ds(at, count)]
        return (
            remote(
                block, sym3.at[2, pl.ds(at, count)], edge_send.at[0], edge_recv.at[0], up
            ),
            remote(
                block, sym3.at[0, pl.ds(at, count)], edge_send.at[1], edge_recv.at[1], down
            ),
        )

    def make_block(s, other):
        base = pl.multiple_of(s * FAR, FAR)
        own = [first[pl.ds(pl.multiple_of(base + i * width, FAR), FAR), :] for i in range(rows)]
        own = jnp.concatenate(own, axis=0)
        sym3[1, s + 1] = (0.5 * (own + other.astype(F32))).astype(BF16)

    mirror[me] = turn(me)
    for far in range(4):
        group = mine ^ far
        count = per if far else per - 1
        some = mirror.at[pl.ds(group * per, count)]
        remote(
            turned.at[pl.ds(group * per, count)], some, turn_send.at[0], turn_recv.at[group],
            lax.rem(me + 1, n),
        ).wait_recv()

        def make(t):
            s = group * per + t
            make_block(s, mirror[s])

        short(per, make)
        to_above, to_below = edge_copies(1 + group * per, per)
        pl.when(has_up)(to_above.start)
        pl.when(has_down)(to_below.start)

    loads[2].wait()
    loads[3].wait()
    group = min(blocks, 16)
    high = group * tile

    def rows_of(strip, start):
        return sym3[strip, pl.ds(start, group)].reshape(high, chans)

    def product(strips, start):
        lhs = [rows_of(k, start + d) for k in strips for d in range(3)]
        rhs = [w2[k, d] for k in strips for d in range(3)]
        return jnp.dot(
            jnp.concatenate(lhs, axis=1), jnp.concatenate(rhs, axis=0),
            preferred_element_type=F32,
        )

    def middle(g):
        acc[pl.ds(pl.multiple_of(g * high, high), high)] = product((1,), g * group)

    loop(blocks // group, middle)
    to_above, to_below = edge_copies(1, n)

    def arrived(strip):
        if strip == 0:
            pl.when(has_up)(to_below.wait_recv)
        else:
            pl.when(has_down)(to_above.wait_recv)

    def finish(strip, g):
        total = acc[pl.ds(pl.multiple_of(g * high, high), high)] + product((strip,), g * group)
        second = jnp.maximum(total, 0.0).astype(BF16)
        side = jnp.dot(second, wp[...], preferred_element_type=F32)
        side = side.reshape(group, rows, FAR, chans)
        part = pl.ds(pl.multiple_of(g * group * FAR, group * FAR), group * FAR)
        for i in range(rows):
            base = xpad[NEAR + i, part].astype(F32)
            out_ref[i, part] = (base + side[:, i].reshape(group * FAR, chans)).astype(BF16)

    def last_strips(early, late):
        arrived(early)

        def add(g):
            span = pl.ds(pl.multiple_of(g * high, high), high)
            acc[span] = acc[span] + product((early,), g * group)

        loop(blocks // group, add)
        arrived(late)
        loop(blocks // group, functools.partial(finish, late))

    pl.when(me % 2 == 0)(lambda: last_strips(2, 0))
    pl.when(me % 2 == 1)(lambda: last_strips(0, 2))

    each_halo(lambda copy: copy.wait_send())
    some = pl.ds(0, n - 1)
    remote(
        turned.at[some], mirror.at[some], turn_send.at[0], turn_recv.at[0], lax.rem(me + 1, n)
    ).wait_send()
    pl.when(has_up)(to_above.wait_send)
    pl.when(has_down)(to_below.wait_send)


def shards(contact_map, first_kernel, second_kernel, project_weight):
    args = (contact_map, first_kernel, second_kernel, project_weight)
    rows, width, chans = contact_map.shape
    n = lax.axis_size("row")
    assert rows == FAR and rows == 2 * NEAR and width == n * rows and n % 4 == 0
    tile = rows * FAR
    blocks = width // FAR
    moved = 9 * chans * chans * 4 + 4 * rows * width * chans
    return pl.pallas_call(
        functools.partial(block_kernel, n),
        out_shape=pltpu.VMEM(contact_map.shape, BF16),
        in_specs=[pl.BlockSpec(memory_space=pltpu.HBM)] * 4,
        out_specs=pl.BlockSpec(memory_space=pltpu.VMEM),
        scratch_shapes=[
            pltpu.VMEM((rows + 2 * NEAR, width, chans), BF16),
            pltpu.VMEM(first_kernel.shape, BF16),
            pltpu.VMEM(second_kernel.shape, BF16),
            pltpu.VMEM(project_weight.shape, BF16),
            pltpu.VMEM((rows * width, chans), F32),
            pltpu.VMEM((n, tile, chans), BF16),
            pltpu.VMEM((n, tile, chans), BF16),
            pltpu.VMEM((3, blocks + 2, tile, chans), BF16),
            pltpu.VMEM((rows * width, chans), F32),
            pltpu.SemaphoreType.DMA((4,)),
            pltpu.SemaphoreType.DMA((2, 2)),
            pltpu.SemaphoreType.DMA((2, 2)),
            pltpu.SemaphoreType.DMA((1,)),
            pltpu.SemaphoreType.DMA((4,)),
            pltpu.SemaphoreType.DMA((2,)),
            pltpu.SemaphoreType.DMA((2,)),
        ],
        compiler_params=pltpu.CompilerParams(
            collective_id=0, has_side_effects=True, vmem_limit_bytes=60 * 1024 * 1024
        ),
        cost_estimate=pl.CostEstimate(
            flops=2 * 19 * rows * width * chans * chans, bytes_accessed=moved, transcendentals=0
        ),
    )(*(pltpu.with_memory_space_constraint(x, pltpu.HBM) for x in args))


def solution(mesh):
    placed = (P(("win", "row"), None, None), P(), P(), P())
    return jax.shard_map(
        shards, mesh=mesh, in_specs=placed, out_specs=P(("win", "row"), None, None), check_vma=False
    )
```

```python
import functools

import jax
import jax.numpy as jnp
from jax import lax
from jax.experimental import pallas as pl
from jax.experimental.pallas import tpu as pltpu
from jax.sharding import PartitionSpec as P

NEAR = 4
FAR = 8
REACH = 16
BF16 = jnp.bfloat16
F32 = jnp.float32


def loop(count, body):
    if count == 1:
        body(0)
    else:
        lax.fori_loop(0, count, lambda i, c: (body(i), c)[1], 0)


def short(count, body):
    if count <= 4:
        for i in range(count):
            body(i)
    else:
        loop(count, body)


def block_kernel(
    n, x_hbm, k1_hbm, k2_hbm, pw_hbm, out_ref,
    xpad, w1, w2, wp, first, turned, mirror, sym3, acc,
    load_sem, halo_send, halo_recv, turn_send, turn_recv, edge_send, edge_recv,
):
    rows, width, chans = x_hbm.shape
    tile = rows * FAR
    blocks = width // FAR
    me = lax.axis_index("row")
    up, down = me - 1, me + 1
    has_up, has_down = me > 0, me < n - 1

    loads = [
        pltpu.make_async_copy(x_hbm, xpad.at[pl.ds(NEAR, rows)], load_sem.at[0]),
        pltpu.make_async_copy(k1_hbm, w1, load_sem.at[1]),
        pltpu.make_async_copy(k2_hbm, w2, load_sem.at[2]),
        pltpu.make_async_copy(pw_hbm, wp, load_sem.at[3]),
    ]
    for load in loads:
        load.start()

    barrier = pltpu.get_barrier_semaphore()

    def greet(k):
        pl.semaphore_signal(
            barrier, inc=1, device_id={"row": lax.rem(me + k + 1, n)},
            device_id_type=pl.DeviceIdType.MESH,
        )

    loop(n - 1, greet)

    zeros = jnp.zeros((tile, chans), BF16)
    for strip in range(3):
        sym3[strip, 0] = zeros
        sym3[strip, blocks + 1] = zeros

    @pl.when(jnp.logical_not(has_up))
    def _():
        xpad[0:NEAR] = jnp.zeros((NEAR, width, chans), BF16)

        def clear(s):
            sym3[0, s + 1] = zeros

        loop(blocks, clear)

    @pl.when(jnp.logical_not(has_down))
    def _():
        xpad[NEAR + rows :] = jnp.zeros((NEAR, width, chans), BF16)

        def clear(s):
            sym3[2, s + 1] = zeros

        loop(blocks, clear)

    def remote(src, dst, send, recv, target):
        return pltpu.make_async_remote_copy(
            src_ref=src, dst_ref=dst, send_sem=send, recv_sem=recv,
            device_id={"row": target}, device_id_type=pl.DeviceIdType.MESH,
        )

    half = n // 2
    cut = width // 2 + REACH
    parts = (((0, cut), (cut, width - cut)), ((width - cut, cut), (0, width - cut)))

    def halo(side, m, which):
        start, size = parts[which][m]
        cols = pl.ds(start, size)
        if side == 0:
            src, dst, target = pl.ds(0, NEAR), pl.ds(NEAR + rows, NEAR), up
        else:
            src, dst, target = pl.ds(rows - NEAR, NEAR), pl.ds(0, NEAR), down
        return remote(
            x_hbm.at[src, cols], xpad.at[dst, cols],
            halo_send.at[side, m], halo_recv.at[side, m], target,
        )

    def each_halo(visit):
        for which in (0, 1):
            for side, there, target in ((0, has_up, up), (1, has_down, down)):
                wanted = (target >= half) if which == 0 else (target < half)

                @pl.when(jnp.logical_and(there, wanted))
                def _():
                    for m in (0, 1):
                        visit(halo(side, m, which))

    pl.semaphore_wait(barrier, n - 1)

    each_halo(lambda copy: copy.start())

    loads[0].wait()
    loads[1].wait()

    step = max(1, min(NEAR, 512 // width))

    def taps(strips, kinds, wide):
        depth = step * wide
        lhs = [strip.reshape(depth, chans) for strip in strips]
        lhs = jnp.concatenate(lhs, axis=1) if len(lhs) > 1 else lhs[0]
        rhs = [jnp.concatenate([w1[k, d] for d in range(3)], axis=1) for k in kinds]
        rhs = jnp.concatenate(rhs, axis=0) if len(rhs) > 1 else rhs[0]
        prod = jnp.dot(lhs, rhs, preferred_element_type=F32)
        column = lax.broadcasted_iota(jnp.int32, (step, wide, chans), 1).reshape(depth, chans)
        left = pltpu.roll(prod[:, :chans], NEAR, 0)
        right = pltpu.roll(prod[:, 2 * chans :], depth - NEAR, 0)
        return (
            prod[:, chans : 2 * chans]
            + jnp.where(column >= NEAR, left, 0.0)
            + jnp.where(column < wide - NEAR, right, 0.0)
        )

    def inner(g):
        a = g * step
        near, mid = xpad[pl.ds(NEAR + a, step)], xpad[pl.ds(2 * NEAR + a, step)]
        high = step * width
        for row, kinds in ((a, (1, 2)), (NEAR + a, (0, 1))):
            first[pl.ds(pl.multiple_of(row * width, width), high)] = taps([near, mid], kinds, width)

    loop(NEAR // step, inner)

    def outer(which, g):
        a = g * step
        keep = width // 2
        start, off = (0, 0) if which == 0 else (width - cut, REACH)
        for row, source, kind in ((a, a, 0), (NEAR + a, rows + NEAR + a, 2)):
            extra = taps([xpad[pl.ds(source, step), pl.ds(start, cut)]], (kind,), cut)
            for i in range(step):
                span = pl.ds(pl.multiple_of((row + i) * width + which * keep, keep), keep)
                total = first[span] + extra[i * cut + off : i * cut + off + keep]
                first[span] = jnp.maximum(total, 0.0).astype(BF16).astype(F32)

    def turn(s):
        base = pl.multiple_of(s * FAR, FAR)
        cols = [first[pl.ds(base + j, rows, stride=width), :] for j in range(FAR)]
        return jnp.concatenate(cols, axis=0).astype(BF16)

    per = n // 4
    mine = me // per

    def turn_copy(s, kind):
        return remote(
            turned.at[s], mirror.at[me], turn_send.at[kind], turn_recv.at[mine], s
        )

    def turn_span(start, count, kind, group):
        some = pl.ds(start, count)
        return remote(
            turned.at[some], mirror.at[some], turn_send.at[kind], turn_recv.at[group],
            lax.rem(me + 1, n),
        )

    def first_half(m, which):
        pl.when(has_up)(halo(1, m, m ^ which).wait_recv)
        pl.when(has_down)(halo(0, m, m ^ which).wait_recv)
        loop(NEAR // step, functools.partial(outer, which))

        for far in (2, 3) if m == 0 else (1, 0):
            group = mine ^ far

            def send_turn(t):
                s = group * per + lax.rem(me + t, per)

                @pl.when(s != me)
                def _():
                    turned[s] = turn(s)
                    if far != 3:
                        turn_copy(s, 0 if far == 2 else 1).start()

            short(per, send_turn)

    @pl.when(me < half)
    def _():
        first_half(0, 1)
        first_half(1, 0)

    @pl.when(me >= half)
    def _():
        first_half(0, 0)
        first_half(1, 1)

    turn_span(0, per, 0, 0).wait_send()

    def send_late(t):
        turn_copy((mine ^ 3) * per + lax.rem(me + t, per), 1).start()

    short(per, send_late)

    def edge_copies(at, count):
        block = sym3.at[1, pl.ds(at, count)]
        return (
            remote(
                block, sym3.at[2, pl.ds(at, count)], edge_send.at[0], edge_recv.at[0], up
            ),
            remote(
                block, sym3.at[0, pl.ds(at, count)], edge_send.at[1], edge_recv.at[1], down
            ),
        )

    def make_block(s, other):
        base = pl.multiple_of(s * FAR, FAR)
        own = [first[pl.ds(pl.multiple_of(base + i * width, FAR), FAR), :] for i in range(rows)]
        own = jnp.concatenate(own, axis=0)
        sym3[1, s + 1] = (0.5 * (own + other.astype(F32))).astype(BF16)

    mirror[me] = turn(me)
    for far in range(4):
        group = mine ^ far
        count = per if far else per - 1
        turn_span(group * per, count, 1, group).wait_recv()

        def make(t):
            s = group * per + t
            make_block(s, mirror[s])

        short(per, make)
        to_above, to_below = edge_copies(1 + group * per, per)
        pl.when(has_up)(to_above.start)
        pl.when(has_down)(to_below.start)

    loads[2].wait()
    loads[3].wait()
    group = min(blocks, 16)
    high = group * tile

    def rows_of(strip, start):
        return sym3[strip, pl.ds(start, group)].reshape(high, chans)

    def product(strips, start):
        lhs = [rows_of(k, start + d) for k in strips for d in range(3)]
        rhs = [w2[k, d] for k in strips for d in range(3)]
        return jnp.dot(
            jnp.concatenate(lhs, axis=1), jnp.concatenate(rhs, axis=0),
            preferred_element_type=F32,
        )

    def middle(g):
        acc[pl.ds(pl.multiple_of(g * high, high), high)] = product((1,), g * group)

    loop(blocks // group, middle)
    to_above, to_below = edge_copies(1, n)

    def arrived(strip):
        if strip == 0:
            pl.when(has_up)(to_below.wait_recv)
        else:
            pl.when(has_down)(to_above.wait_recv)

    def finish(strip, g):
        total = acc[pl.ds(pl.multiple_of(g * high, high), high)] + product((strip,), g * group)
        second = jnp.maximum(total, 0.0).astype(BF16)
        side = jnp.dot(second, wp[...], preferred_element_type=F32)
        side = side.reshape(group, rows, FAR, chans)
        part = pl.ds(pl.multiple_of(g * group * FAR, group * FAR), group * FAR)
        for i in range(rows):
            base = xpad[NEAR + i, part].astype(F32)
            out_ref[i, part] = (base + side[:, i].reshape(group * FAR, chans)).astype(BF16)

    def last_strips(early, late):
        arrived(early)

        def add(g):
            span = pl.ds(pl.multiple_of(g * high, high), high)
            acc[span] = acc[span] + product((early,), g * group)

        loop(blocks // group, add)
        arrived(late)
        loop(blocks // group, functools.partial(finish, late))

    pl.when(me % 2 == 0)(lambda: last_strips(2, 0))
    pl.when(me % 2 == 1)(lambda: last_strips(0, 2))

    each_halo(lambda copy: copy.wait_send())
    turn_span(0, n - 1 - per, 1, 0).wait_send()
    pl.when(has_up)(to_above.wait_send)
    pl.when(has_down)(to_below.wait_send)


def shards(contact_map, first_kernel, second_kernel, project_weight):
    args = (contact_map, first_kernel, second_kernel, project_weight)
    rows, width, chans = contact_map.shape
    n = lax.axis_size("row")
    assert rows == FAR and rows == 2 * NEAR and width == n * rows and n % 4 == 0
    tile = rows * FAR
    blocks = width // FAR
    moved = 9 * chans * chans * 4 + 4 * rows * width * chans
    return pl.pallas_call(
        functools.partial(block_kernel, n),
        out_shape=pltpu.VMEM(contact_map.shape, BF16),
        in_specs=[pl.BlockSpec(memory_space=pltpu.HBM)] * 4,
        out_specs=pl.BlockSpec(memory_space=pltpu.VMEM),
        scratch_shapes=[
            pltpu.VMEM((rows + 2 * NEAR, width, chans), BF16),
            pltpu.VMEM(first_kernel.shape, BF16),
            pltpu.VMEM(second_kernel.shape, BF16),
            pltpu.VMEM(project_weight.shape, BF16),
            pltpu.VMEM((rows * width, chans), F32),
            pltpu.VMEM((n, tile, chans), BF16),
            pltpu.VMEM((n, tile, chans), BF16),
            pltpu.VMEM((3, blocks + 2, tile, chans), BF16),
            pltpu.VMEM((rows * width, chans), F32),
            pltpu.SemaphoreType.DMA((4,)),
            pltpu.SemaphoreType.DMA((2, 2)),
            pltpu.SemaphoreType.DMA((2, 2)),
            pltpu.SemaphoreType.DMA((2,)),
            pltpu.SemaphoreType.DMA((4,)),
            pltpu.SemaphoreType.DMA((2,)),
            pltpu.SemaphoreType.DMA((2,)),
        ],
        compiler_params=pltpu.CompilerParams(
            collective_id=0, has_side_effects=True, vmem_limit_bytes=60 * 1024 * 1024
        ),
        cost_estimate=pl.CostEstimate(
            flops=2 * 19 * rows * width * chans * chans, bytes_accessed=moved, transcendentals=0
        ),
    )(*(pltpu.with_memory_space_constraint(x, pltpu.HBM) for x in args))


def solution(mesh):
    placed = (P(("win", "row"), None, None), P(), P(), P())
    return jax.shard_map(
        shards, mesh=mesh, in_specs=placed, out_specs=P(("win", "row"), None, None), check_vma=False
    )
```

```python
import functools

import jax
import jax.numpy as jnp
from jax import lax
from jax.experimental import pallas as pl
from jax.experimental.pallas import tpu as pltpu
from jax.sharding import PartitionSpec as P

NEAR = 4
FAR = 8
REACH = 16
BF16 = jnp.bfloat16
F32 = jnp.float32


def loop(count, body):
    if count == 1:
        body(0)
    else:
        lax.fori_loop(0, count, lambda i, c: (body(i), c)[1], 0)


def short(count, body):
    if count <= 4:
        for i in range(count):
            body(i)
    else:
        loop(count, body)


def block_kernel(
    n, x_hbm, k1_hbm, k2_hbm, pw_hbm, out_ref,
    xpad, w1, w2, wp, first, turned, mirror, sym3, acc,
    load_sem, halo_send, halo_recv, turn_send, turn_recv, edge_send, edge_recv,
):
    rows, width, chans = x_hbm.shape
    tile = rows * FAR
    blocks = width // FAR
    me = lax.axis_index("row")
    up, down = me - 1, me + 1
    has_up, has_down = me > 0, me < n - 1

    loads = [
        pltpu.make_async_copy(x_hbm, xpad.at[pl.ds(NEAR, rows)], load_sem.at[0]),
        pltpu.make_async_copy(k1_hbm, w1, load_sem.at[1]),
        pltpu.make_async_copy(k2_hbm, w2, load_sem.at[2]),
        pltpu.make_async_copy(pw_hbm, wp, load_sem.at[3]),
    ]
    for load in loads:
        load.start()

    barrier = pltpu.get_barrier_semaphore()

    def greet(k):
        pl.semaphore_signal(
            barrier, inc=1, device_id={"row": lax.rem(me + k + 1, n)},
            device_id_type=pl.DeviceIdType.MESH,
        )

    loop(n - 1, greet)

    zeros = jnp.zeros((tile, chans), BF16)
    for strip in range(3):
        sym3[strip, 0] = zeros
        sym3[strip, blocks + 1] = zeros

    @pl.when(jnp.logical_not(has_up))
    def _():
        xpad[0:NEAR] = jnp.zeros((NEAR, width, chans), BF16)

        def clear(s):
            sym3[0, s + 1] = zeros

        loop(blocks, clear)

    @pl.when(jnp.logical_not(has_down))
    def _():
        xpad[NEAR + rows :] = jnp.zeros((NEAR, width, chans), BF16)

        def clear(s):
            sym3[2, s + 1] = zeros

        loop(blocks, clear)

    def remote(src, dst, send, recv, target):
        return pltpu.make_async_remote_copy(
            src_ref=src, dst_ref=dst, send_sem=send, recv_sem=recv,
            device_id={"row": target}, device_id_type=pl.DeviceIdType.MESH,
        )

    half = n // 2
    per = n // 4
    mine = me // per
    keep = width // 4
    edges = [0] + [c * keep + REACH for c in (1, 2, 3)] + [width]
    rising = [(edges[m], edges[m + 1] - edges[m]) for m in range(4)]
    falling = [(width - start - size, size) for start, size in rising]
    parts = (rising, falling)

    def halo(side, m, which):
        start, size = parts[which][m]
        cols = pl.ds(start, size)
        if side == 0:
            src, dst, target = pl.ds(0, NEAR), pl.ds(NEAR + rows, NEAR), up
        else:
            src, dst, target = pl.ds(rows - NEAR, NEAR), pl.ds(0, NEAR), down
        return remote(
            x_hbm.at[src, cols], xpad.at[dst, cols],
            halo_send.at[side, m], halo_recv.at[side, m], target,
        )

    def each_halo(visit):
        for which in (0, 1):
            for side, there, target in ((0, has_up, up), (1, has_down, down)):
                wanted = (target >= half) if which == 0 else (target < half)

                @pl.when(jnp.logical_and(there, wanted))
                def _():
                    for m in range(4):
                        visit(halo(side, m, which))

    pl.semaphore_wait(barrier, n - 1)

    each_halo(lambda copy: copy.start())

    loads[0].wait()
    loads[1].wait()

    step = max(1, min(NEAR, 512 // width))

    def taps(strips, kinds, wide):
        depth = step * wide
        lhs = [strip.reshape(depth, chans) for strip in strips]
        lhs = jnp.concatenate(lhs, axis=1) if len(lhs) > 1 else lhs[0]
        rhs = [jnp.concatenate([w1[k, d] for d in range(3)], axis=1) for k in kinds]
        rhs = jnp.concatenate(rhs, axis=0) if len(rhs) > 1 else rhs[0]
        prod = jnp.dot(lhs, rhs, preferred_element_type=F32)
        column = lax.broadcasted_iota(jnp.int32, (step, wide, chans), 1).reshape(depth, chans)
        left = pltpu.roll(prod[:, :chans], NEAR, 0)
        right = pltpu.roll(prod[:, 2 * chans :], depth - NEAR, 0)
        return (
            prod[:, chans : 2 * chans]
            + jnp.where(column >= NEAR, left, 0.0)
            + jnp.where(column < wide - NEAR, right, 0.0)
        )

    def inner(g):
        a = g * step
        near, mid = xpad[pl.ds(NEAR + a, step)], xpad[pl.ds(2 * NEAR + a, step)]
        high = step * width
        for row, kinds in ((a, (1, 2)), (NEAR + a, (0, 1))):
            first[pl.ds(pl.multiple_of(row * width, width), high)] = taps([near, mid], kinds, width)

    loop(NEAR // step, inner)

    def outer(c, g):
        a = g * step
        start = max(0, c * keep - REACH)
        off = c * keep - start
        wide = min(width, (c + 1) * keep + REACH) - start
        for row, source, kind in ((a, a, 0), (NEAR + a, rows + NEAR + a, 2)):
            extra = taps([xpad[pl.ds(source, step), pl.ds(start, wide)]], (kind,), wide)
            for i in range(step):
                span = pl.ds(pl.multiple_of((row + i) * width + c * keep, keep), keep)
                total = first[span] + extra[i * wide + off : i * wide + off + keep]
                first[span] = jnp.maximum(total, 0.0).astype(BF16).astype(F32)

    def turn(s):
        base = pl.multiple_of(s * FAR, FAR)
        cols = [first[pl.ds(base + j, rows, stride=width), :] for j in range(FAR)]
        return jnp.concatenate(cols, axis=0).astype(BF16)

    def turn_copy(s, kind):
        return remote(
            turned.at[s], mirror.at[me], turn_send.at[kind], turn_recv.at[mine], s
        )

    def turn_span(start, count, kind, group):
        some = pl.ds(start, count)
        return remote(
            turned.at[some], mirror.at[some], turn_send.at[kind], turn_recv.at[group],
            lax.rem(me + 1, n),
        )

    def first_quarter(m, which):
        c = 3 - m if which else m
        pl.when(has_up)(halo(1, m, which).wait_recv)
        pl.when(has_down)(halo(0, m, which).wait_recv)
        loop(NEAR // step, functools.partial(outer, c))

        def make_turn(t):
            s = c * per + lax.rem(me + t, per)
            turned[s] = turn(s)

        short(per, make_turn)

        def send_group(kind):
            def send(t):
                s = c * per + lax.rem(me + t, per)
                pl.when(s != me)(lambda: turn_copy(s, kind).start())

            short(per, send)

        pl.when(mine == c ^ 2)(lambda: send_group(0))
        pl.when(jnp.logical_and(mine != c ^ 2, mine != c ^ 3))(lambda: send_group(1))

    @pl.when(me < half)
    def _():
        for m in range(4):
            first_quarter(m, 1)

    @pl.when(me >= half)
    def _():
        for m in range(4):
            first_quarter(m, 0)

    turn_span(0, per, 0, 0).wait_send()

    def send_late(t):
        turn_copy((mine ^ 3) * per + lax.rem(me + t, per), 1).start()

    short(per, send_late)

    def edge_copies(at, count):
        block = sym3.at[1, pl.ds(at, count)]
        return (
            remote(
                block, sym3.at[2, pl.ds(at, count)], edge_send.at[0], edge_recv.at[0], up
            ),
            remote(
                block, sym3.at[0, pl.ds(at, count)], edge_send.at[1], edge_recv.at[1], down
            ),
        )

    def make_block(s, other):
        base = pl.multiple_of(s * FAR, FAR)
        own = [first[pl.ds(pl.multiple_of(base + i * width, FAR), FAR), :] for i in range(rows)]
        own = jnp.concatenate(own, axis=0)
        sym3[1, s + 1] = (0.5 * (own + other.astype(F32))).astype(BF16)

    mirror[me] = turned[me]
    for far in range(4):
        group = mine ^ far
        count = per if far else per - 1
        turn_span(group * per, count, 1, group).wait_recv()

        def make(t):
            s = group * per + t
            make_block(s, mirror[s])

        short(per, make)
        to_above, to_below = edge_copies(1 + group * per, per)
        pl.when(has_up)(to_above.start)
        pl.when(has_down)(to_below.start)

    loads[2].wait()
    loads[3].wait()
    group = min(blocks, 16)
    high = group * tile

    def rows_of(strip, start):
        return sym3[strip, pl.ds(start, group)].reshape(high, chans)

    def product(strips, start):
        lhs = [rows_of(k, start + d) for k in strips for d in range(3)]
        rhs = [w2[k, d] for k in strips for d in range(3)]
        return jnp.dot(
            jnp.concatenate(lhs, axis=1), jnp.concatenate(rhs, axis=0),
            preferred_element_type=F32,
        )

    def middle(g):
        acc[pl.ds(pl.multiple_of(g * high, high), high)] = product((1,), g * group)

    loop(blocks // group, middle)
    to_above, to_below = edge_copies(1, n)

    def arrived(strip):
        if strip == 0:
            pl.when(has_up)(to_below.wait_recv)
        else:
            pl.when(has_down)(to_above.wait_recv)

    def finish(strip, g):
        total = acc[pl.ds(pl.multiple_of(g * high, high), high)] + product((strip,), g * group)
        second = jnp.maximum(total, 0.0).astype(BF16)
        side = jnp.dot(second, wp[...], preferred_element_type=F32)
        side = side.reshape(group, rows, FAR, chans)
        part = pl.ds(pl.multiple_of(g * group * FAR, group * FAR), group * FAR)
        for i in range(rows):
            base = xpad[NEAR + i, part].astype(F32)
            out_ref[i, part] = (base + side[:, i].reshape(group * FAR, chans)).astype(BF16)

    def last_strips(early, late):
        arrived(early)

        def add(g):
            span = pl.ds(pl.multiple_of(g * high, high), high)
            acc[span] = acc[span] + product((early,), g * group)

        loop(blocks // group, add)
        arrived(late)
        loop(blocks // group, functools.partial(finish, late))

    pl.when(me % 2 == 0)(lambda: last_strips(2, 0))
    pl.when(me % 2 == 1)(lambda: last_strips(0, 2))

    each_halo(lambda copy: copy.wait_send())
    turn_span(0, n - 1 - per, 1, 0).wait_send()
    pl.when(has_up)(to_above.wait_send)
    pl.when(has_down)(to_below.wait_send)


def shards(contact_map, first_kernel, second_kernel, project_weight):
    args = (contact_map, first_kernel, second_kernel, project_weight)
    rows, width, chans = contact_map.shape
    n = lax.axis_size("row")
    assert rows == FAR and rows == 2 * NEAR and width == n * rows and n % 4 == 0
    tile = rows * FAR
    blocks = width // FAR
    moved = 9 * chans * chans * 4 + 4 * rows * width * chans
    return pl.pallas_call(
        functools.partial(block_kernel, n),
        out_shape=pltpu.VMEM(contact_map.shape, BF16),
        in_specs=[pl.BlockSpec(memory_space=pltpu.HBM)] * 4,
        out_specs=pl.BlockSpec(memory_space=pltpu.VMEM),
        scratch_shapes=[
            pltpu.VMEM((rows + 2 * NEAR, width, chans), BF16),
            pltpu.VMEM(first_kernel.shape, BF16),
            pltpu.VMEM(second_kernel.shape, BF16),
            pltpu.VMEM(project_weight.shape, BF16),
            pltpu.VMEM((rows * width, chans), F32),
            pltpu.VMEM((n, tile, chans), BF16),
            pltpu.VMEM((n, tile, chans), BF16),
            pltpu.VMEM((3, blocks + 2, tile, chans), BF16),
            pltpu.VMEM((rows * width, chans), F32),
            pltpu.SemaphoreType.DMA((4,)),
            pltpu.SemaphoreType.DMA((2, 4)),
            pltpu.SemaphoreType.DMA((2, 4)),
            pltpu.SemaphoreType.DMA((2,)),
            pltpu.SemaphoreType.DMA((4,)),
            pltpu.SemaphoreType.DMA((2,)),
            pltpu.SemaphoreType.DMA((2,)),
        ],
        compiler_params=pltpu.CompilerParams(
            collective_id=0, has_side_effects=True, vmem_limit_bytes=60 * 1024 * 1024
        ),
        cost_estimate=pl.CostEstimate(
            flops=2 * 19 * rows * width * chans * chans, bytes_accessed=moved, transcendentals=0
        ),
    )(*(pltpu.with_memory_space_constraint(x, pltpu.HBM) for x in args))


def solution(mesh):
    placed = (P(("win", "row"), None, None), P(), P(), P())
    return jax.shard_map(
        shards, mesh=mesh, in_specs=placed, out_specs=P(("win", "row"), None, None), check_vma=False
    )
```

```python
import functools

import jax
import jax.numpy as jnp
from jax import lax
from jax.experimental import pallas as pl
from jax.experimental.pallas import tpu as pltpu
from jax.sharding import PartitionSpec as P

NEAR = 4
FAR = 8
REACH = 16
BF16 = jnp.bfloat16
F32 = jnp.float32


def loop(count, body):
    if count == 1:
        body(0)
    else:
        lax.fori_loop(0, count, lambda i, c: (body(i), c)[1], 0)


def short(count, body):
    if count <= 4:
        for i in range(count):
            body(i)
    else:
        loop(count, body)


def block_kernel(
    n, x_hbm, k1_hbm, k2_hbm, pw_hbm, out_ref,
    xpad, w1, w2, wp, first, turned, mirror, sym3, acc,
    load_sem, halo_send, halo_recv, turn_send, turn_recv, edge_send, edge_recv,
):
    rows, width, chans = x_hbm.shape
    tile = rows * FAR
    blocks = width // FAR
    me = lax.axis_index("row")
    up, down = me - 1, me + 1
    has_up, has_down = me > 0, me < n - 1

    loads = [
        pltpu.make_async_copy(x_hbm, xpad.at[pl.ds(NEAR, rows)], load_sem.at[0]),
        pltpu.make_async_copy(k1_hbm, w1, load_sem.at[1]),
        pltpu.make_async_copy(k2_hbm, w2, load_sem.at[2]),
        pltpu.make_async_copy(pw_hbm, wp, load_sem.at[3]),
    ]
    for load in loads:
        load.start()

    barrier = pltpu.get_barrier_semaphore()

    def greet(k):
        pl.semaphore_signal(
            barrier, inc=1, device_id={"row": lax.rem(me + k + 1, n)},
            device_id_type=pl.DeviceIdType.MESH,
        )

    loop(n - 1, greet)

    zeros = jnp.zeros((tile, chans), BF16)
    for strip in range(3):
        sym3[strip, 0] = zeros
        sym3[strip, blocks + 1] = zeros

    @pl.when(jnp.logical_not(has_up))
    def _():
        xpad[0:NEAR] = jnp.zeros((NEAR, width, chans), BF16)

        def clear(s):
            sym3[0, s + 1] = zeros

        loop(blocks, clear)

    @pl.when(jnp.logical_not(has_down))
    def _():
        xpad[NEAR + rows :] = jnp.zeros((NEAR, width, chans), BF16)

        def clear(s):
            sym3[2, s + 1] = zeros

        loop(blocks, clear)

    def remote(src, dst, send, recv, target):
        return pltpu.make_async_remote_copy(
            src_ref=src, dst_ref=dst, send_sem=send, recv_sem=recv,
            device_id={"row": target}, device_id_type=pl.DeviceIdType.MESH,
        )

    half = n // 2
    per = n // 4
    mine = me // per
    keep = width // 4
    edges = [0] + [c * keep + REACH for c in (1, 2, 3)] + [width]
    rising = [(edges[m], edges[m + 1] - edges[m]) for m in range(4)]
    falling = [(width - start - size, size) for start, size in rising]
    parts = (rising, falling)

    def halo(side, m, which):
        start, size = parts[which][m]
        cols = pl.ds(start, size)
        if side == 0:
            src, dst, target = pl.ds(0, NEAR), pl.ds(NEAR + rows, NEAR), up
        else:
            src, dst, target = pl.ds(rows - NEAR, NEAR), pl.ds(0, NEAR), down
        return remote(
            x_hbm.at[src, cols], xpad.at[dst, cols],
            halo_send.at[side, m], halo_recv.at[side, m], target,
        )

    def each_halo(parts_of, visit):
        for which in (0, 1):
            for side, there, target in ((0, has_up, up), (1, has_down, down)):
                wanted = (target >= half) if which == 0 else (target < half)

                @pl.when(jnp.logical_and(there, wanted))
                def _():
                    for m in parts_of:
                        visit(halo(side, m, which))

    pl.semaphore_wait(barrier, n - 1)

    each_halo((0,), lambda copy: copy.start())

    loads[0].wait()
    loads[1].wait()

    step = max(1, min(NEAR, 512 // width))

    def taps(strips, kinds, wide):
        depth = step * wide
        lhs = [strip.reshape(depth, chans) for strip in strips]
        lhs = jnp.concatenate(lhs, axis=1) if len(lhs) > 1 else lhs[0]
        rhs = [jnp.concatenate([w1[k, d] for d in range(3)], axis=1) for k in kinds]
        rhs = jnp.concatenate(rhs, axis=0) if len(rhs) > 1 else rhs[0]
        prod = jnp.dot(lhs, rhs, preferred_element_type=F32)
        column = lax.broadcasted_iota(jnp.int32, (step, wide, chans), 1).reshape(depth, chans)
        left = pltpu.roll(prod[:, :chans], NEAR, 0)
        right = pltpu.roll(prod[:, 2 * chans :], depth - NEAR, 0)
        return (
            prod[:, chans : 2 * chans]
            + jnp.where(column >= NEAR, left, 0.0)
            + jnp.where(column < wide - NEAR, right, 0.0)
        )

    def inner(shift, kinds, g):
        a = g * step
        near, mid = xpad[pl.ds(NEAR + a, step)], xpad[pl.ds(2 * NEAR + a, step)]
        row = shift + a
        first[pl.ds(pl.multiple_of(row * width, width), step * width)] = taps(
            [near, mid], kinds, width
        )

    loop(NEAR // step, functools.partial(inner, 0, (1, 2)))
    each_halo((1,), lambda copy: copy.start())
    loop(NEAR // step, functools.partial(inner, NEAR, (0, 1)))
    each_halo((2, 3), lambda copy: copy.start())

    def outer(c, g):
        a = g * step
        start = max(0, c * keep - REACH)
        off = c * keep - start
        wide = min(width, (c + 1) * keep + REACH) - start
        for row, source, kind in ((a, a, 0), (NEAR + a, rows + NEAR + a, 2)):
            extra = taps([xpad[pl.ds(source, step), pl.ds(start, wide)]], (kind,), wide)
            for i in range(step):
                span = pl.ds(pl.multiple_of((row + i) * width + c * keep, keep), keep)
                total = first[span] + extra[i * wide + off : i * wide + off + keep]
                first[span] = jnp.maximum(total, 0.0).astype(BF16).astype(F32)

    def turn(s):
        base = pl.multiple_of(s * FAR, FAR)
        cols = [first[pl.ds(base + j, rows, stride=width), :] for j in range(FAR)]
        return jnp.concatenate(cols, axis=0).astype(BF16)

    def turn_copy(s, kind):
        return remote(
            turned.at[s], mirror.at[me], turn_send.at[kind], turn_recv.at[mine], s
        )

    def turn_span(start, count, kind, group):
        some = pl.ds(start, count)
        return remote(
            turned.at[some], mirror.at[some], turn_send.at[kind], turn_recv.at[group],
            lax.rem(me + 1, n),
        )

    def first_quarter(m, which):
        c = 3 - m if which else m
        pl.when(has_up)(halo(1, m, which).wait_recv)
        pl.when(has_down)(halo(0, m, which).wait_recv)
        loop(NEAR // step, functools.partial(outer, c))

        def make_turn(t):
            s = c * per + lax.rem(me + t, per)
            turned[s] = turn(s)

        short(per, make_turn)

        def send_group(kind):
            def send(t):
                s = c * per + lax.rem(me + t, per)
                pl.when(s != me)(lambda: turn_copy(s, kind).start())

            short(per, send)

        pl.when(mine == c ^ 2)(lambda: send_group(0))
        pl.when(jnp.logical_and(mine != c ^ 2, mine != c ^ 3))(lambda: send_group(1))

    @pl.when(me < half)
    def _():
        for m in range(4):
            first_quarter(m, 1)

    @pl.when(me >= half)
    def _():
        for m in range(4):
            first_quarter(m, 0)

    def send_late(t):
        turn_copy((mine ^ 3) * per + lax.rem(me + t, per), 1).start()

    short(per, send_late)

    def edge_copies(at, count):
        block = sym3.at[1, pl.ds(at, count)]
        return (
            remote(
                block, sym3.at[2, pl.ds(at, count)], edge_send.at[0], edge_recv.at[0], up
            ),
            remote(
                block, sym3.at[0, pl.ds(at, count)], edge_send.at[1], edge_recv.at[1], down
            ),
        )

    def make_block(s, other):
        base = pl.multiple_of(s * FAR, FAR)
        own = [first[pl.ds(pl.multiple_of(base + i * width, FAR), FAR), :] for i in range(rows)]
        own = jnp.concatenate(own, axis=0)
        sym3[1, s + 1] = (0.5 * (own + other.astype(F32))).astype(BF16)

    mirror[me] = turned[me]
    for far in range(4):
        group = mine ^ far
        count = per if far else per - 1
        turn_span(group * per, count, 1, group).wait_recv()

        def make(t):
            s = group * per + t
            make_block(s, mirror[s])

        short(per, make)
        to_above, to_below = edge_copies(1 + group * per, per)
        pl.when(has_up)(to_above.start)
        pl.when(has_down)(to_below.start)

    loads[2].wait()
    loads[3].wait()
    group = min(blocks, 16)
    high = group * tile

    def rows_of(strip, start):
        return sym3[strip, pl.ds(start, group)].reshape(high, chans)

    def product(strips, start):
        lhs = [rows_of(k, start + d) for k in strips for d in range(3)]
        rhs = [w2[k, d] for k in strips for d in range(3)]
        return jnp.dot(
            jnp.concatenate(lhs, axis=1), jnp.concatenate(rhs, axis=0),
            preferred_element_type=F32,
        )

    def middle(g):
        acc[pl.ds(pl.multiple_of(g * high, high), high)] = product((1,), g * group)

    loop(blocks // group, middle)
    to_above, to_below = edge_copies(1, n)

    def arrived(strip):
        if strip == 0:
            pl.when(has_up)(to_below.wait_recv)
        else:
            pl.when(has_down)(to_above.wait_recv)

    def finish(strip, g):
        total = acc[pl.ds(pl.multiple_of(g * high, high), high)] + product((strip,), g * group)
        second = jnp.maximum(total, 0.0).astype(BF16)
        side = jnp.dot(second, wp[...], preferred_element_type=F32)
        side = side.reshape(group, rows, FAR, chans)
        part = pl.ds(pl.multiple_of(g * group * FAR, group * FAR), group * FAR)
        for i in range(rows):
            base = xpad[NEAR + i, part].astype(F32)
            out_ref[i, part] = (base + side[:, i].reshape(group * FAR, chans)).astype(BF16)

    def last_strips(early, late):
        arrived(early)

        def add(g):
            span = pl.ds(pl.multiple_of(g * high, high), high)
            acc[span] = acc[span] + product((early,), g * group)

        loop(blocks // group, add)
        arrived(late)
        loop(blocks // group, functools.partial(finish, late))

    pl.when(me % 2 == 0)(lambda: last_strips(2, 0))
    pl.when(me % 2 == 1)(lambda: last_strips(0, 2))

    each_halo(range(4), lambda copy: copy.wait_send())
    turn_span(0, per, 0, 0).wait_send()
    turn_span(0, n - 1 - per, 1, 0).wait_send()
    pl.when(has_up)(to_above.wait_send)
    pl.when(has_down)(to_below.wait_send)


def shards(contact_map, first_kernel, second_kernel, project_weight):
    args = (contact_map, first_kernel, second_kernel, project_weight)
    rows, width, chans = contact_map.shape
    n = lax.axis_size("row")
    assert rows == FAR and rows == 2 * NEAR and width == n * rows and n % 4 == 0
    tile = rows * FAR
    blocks = width // FAR
    moved = 9 * chans * chans * 4 + 4 * rows * width * chans
    return pl.pallas_call(
        functools.partial(block_kernel, n),
        out_shape=pltpu.VMEM(contact_map.shape, BF16),
        in_specs=[pl.BlockSpec(memory_space=pltpu.HBM)] * 4,
        out_specs=pl.BlockSpec(memory_space=pltpu.VMEM),
        scratch_shapes=[
            pltpu.VMEM((rows + 2 * NEAR, width, chans), BF16),
            pltpu.VMEM(first_kernel.shape, BF16),
            pltpu.VMEM(second_kernel.shape, BF16),
            pltpu.VMEM(project_weight.shape, BF16),
            pltpu.VMEM((rows * width, chans), F32),
            pltpu.VMEM((n, tile, chans), BF16),
            pltpu.VMEM((n, tile, chans), BF16),
            pltpu.VMEM((3, blocks + 2, tile, chans), BF16),
            pltpu.VMEM((rows * width, chans), F32),
            pltpu.SemaphoreType.DMA((4,)),
            pltpu.SemaphoreType.DMA((2, 4)),
            pltpu.SemaphoreType.DMA((2, 4)),
            pltpu.SemaphoreType.DMA((2,)),
            pltpu.SemaphoreType.DMA((4,)),
            pltpu.SemaphoreType.DMA((2,)),
            pltpu.SemaphoreType.DMA((2,)),
        ],
        compiler_params=pltpu.CompilerParams(
            collective_id=0, has_side_effects=True, vmem_limit_bytes=60 * 1024 * 1024
        ),
        cost_estimate=pl.CostEstimate(
            flops=2 * 19 * rows * width * chans * chans, bytes_accessed=moved, transcendentals=0
        ),
    )(*(pltpu.with_memory_space_constraint(x, pltpu.HBM) for x in args))


def solution(mesh):
    placed = (P(("win", "row"), None, None), P(), P(), P())
    return jax.shard_map(
        shards, mesh=mesh, in_specs=placed, out_specs=P(("win", "row"), None, None), check_vma=False
    )
```

```python
import functools

import jax
import jax.numpy as jnp
from jax import lax
from jax.experimental import pallas as pl
from jax.experimental.pallas import tpu as pltpu
from jax.sharding import PartitionSpec as P

NEAR = 4
FAR = 8
REACH = 16
BF16 = jnp.bfloat16
F32 = jnp.float32


def loop(count, body):
    if count == 1:
        body(0)
    else:
        lax.fori_loop(0, count, lambda i, c: (body(i), c)[1], 0)


def short(count, body):
    if count <= 4:
        for i in range(count):
            body(i)
    else:
        loop(count, body)


def block_kernel(
    n, x_hbm, k1_hbm, k2_hbm, pw_hbm, out_ref,
    xpad, w1, w2, wp, first, turned, mirror, sym3, acc, staged, flip,
    load_sem, halo_send, halo_recv, turn_send, turn_recv, edge_send, edge_recv, direct_send,
):
    rows, width, chans = x_hbm.shape
    tile = rows * FAR
    blocks = width // FAR
    me = lax.axis_index("row")
    up, down = me - 1, me + 1
    has_up, has_down = me > 0, me < n - 1

    loads = [
        pltpu.make_async_copy(x_hbm, xpad.at[pl.ds(NEAR, rows)], load_sem.at[0]),
        pltpu.make_async_copy(k1_hbm, w1, load_sem.at[1]),
        pltpu.make_async_copy(k2_hbm, w2, load_sem.at[2]),
        pltpu.make_async_copy(pw_hbm, wp, load_sem.at[3]),
    ]
    for load in loads:
        load.start()

    barrier = pltpu.get_barrier_semaphore()

    def greet(k):
        pl.semaphore_signal(
            barrier, inc=1, device_id={"row": lax.rem(me + k + 1, n)},
            device_id_type=pl.DeviceIdType.MESH,
        )

    loop(n - 1, greet)

    zeros = jnp.zeros((tile, chans), BF16)
    for strip in range(3):
        sym3[strip, 0] = zeros
        sym3[strip, blocks + 1] = zeros

    @pl.when(jnp.logical_not(has_up))
    def _():
        xpad[0:NEAR] = jnp.zeros((NEAR, width, chans), BF16)

        def clear(s):
            sym3[0, s + 1] = zeros

        loop(blocks, clear)

    @pl.when(jnp.logical_not(has_down))
    def _():
        xpad[NEAR + rows :] = jnp.zeros((NEAR, width, chans), BF16)

        def clear(s):
            sym3[2, s + 1] = zeros

        loop(blocks, clear)

    def remote(src, dst, send, recv, target):
        return pltpu.make_async_remote_copy(
            src_ref=src, dst_ref=dst, send_sem=send, recv_sem=recv,
            device_id={"row": target}, device_id_type=pl.DeviceIdType.MESH,
        )

    half = n // 2
    per = n // 4
    mine = me // per
    keep = width // 4
    edges = [0] + [c * keep + REACH for c in (1, 2, 3)] + [width]
    rising = [(edges[m], edges[m + 1] - edges[m]) for m in range(4)]
    falling = [(width - start - size, size) for start, size in rising]
    parts = (rising, falling)

    def halo(side, m, which):
        start, size = parts[which][m]
        cols = pl.ds(start, size)
        if side == 0:
            src, dst, target = pl.ds(0, NEAR), pl.ds(NEAR + rows, NEAR), up
        else:
            src, dst, target = pl.ds(rows - NEAR, NEAR), pl.ds(0, NEAR), down
        return remote(
            x_hbm.at[src, cols], xpad.at[dst, cols],
            halo_send.at[side, m], halo_recv.at[side, m], target,
        )

    def each_halo(parts_of, visit):
        for which in (0, 1):
            for side, there, target in ((0, has_up, up), (1, has_down, down)):
                wanted = (target >= half) if which == 0 else (target < half)

                @pl.when(jnp.logical_and(there, wanted))
                def _():
                    for m in parts_of:
                        visit(halo(side, m, which))

    pl.semaphore_wait(barrier, n - 1)

    each_halo((0,), lambda copy: copy.start())

    loads[0].wait()
    loads[1].wait()

    step = max(1, min(NEAR, 512 // width))

    def taps(strips, kinds, wide):
        depth = step * wide
        lhs = [strip.reshape(depth, chans) for strip in strips]
        lhs = jnp.concatenate(lhs, axis=1) if len(lhs) > 1 else lhs[0]
        rhs = [jnp.concatenate([w1[k, d] for d in range(3)], axis=1) for k in kinds]
        rhs = jnp.concatenate(rhs, axis=0) if len(rhs) > 1 else rhs[0]
        prod = jnp.dot(lhs, rhs, preferred_element_type=F32)
        column = lax.broadcasted_iota(jnp.int32, (step, wide, chans), 1).reshape(depth, chans)
        left = pltpu.roll(prod[:, :chans], NEAR, 0)
        right = pltpu.roll(prod[:, 2 * chans :], depth - NEAR, 0)
        return (
            prod[:, chans : 2 * chans]
            + jnp.where(column >= NEAR, left, 0.0)
            + jnp.where(column < wide - NEAR, right, 0.0)
        )

    def inner(shift, kinds, g):
        a = g * step
        near, mid = xpad[pl.ds(NEAR + a, step)], xpad[pl.ds(2 * NEAR + a, step)]
        row = shift + a
        first[pl.ds(pl.multiple_of(row * width, width), step * width)] = taps(
            [near, mid], kinds, width
        )

    loop(NEAR // step, functools.partial(inner, 0, (1, 2)))
    each_halo((1,), lambda copy: copy.start())
    loop(NEAR // step, functools.partial(inner, NEAR, (0, 1)))
    each_halo((2, 3), lambda copy: copy.start())

    def outer(c, g):
        a = g * step
        start = max(0, c * keep - REACH)
        off = c * keep - start
        wide = min(width, (c + 1) * keep + REACH) - start
        for row, source, kind in ((a, a, 0), (NEAR + a, rows + NEAR + a, 2)):
            extra = taps([xpad[pl.ds(source, step), pl.ds(start, wide)]], (kind,), wide)
            for i in range(step):
                span = pl.ds(pl.multiple_of((row + i) * width + c * keep, keep), keep)
                total = first[span] + extra[i * wide + off : i * wide + off + keep]
                first[span] = jnp.maximum(total, 0.0).astype(BF16).astype(F32)

    def turn(s):
        base = pl.multiple_of(s * FAR, FAR)
        cols = [first[pl.ds(base + j, rows, stride=width), :] for j in range(FAR)]
        return jnp.concatenate(cols, axis=0).astype(BF16)

    def turn_copy(s, kind):
        return remote(
            turned.at[s], mirror.at[me], turn_send.at[kind], turn_recv.at[mine], s
        )

    def turn_span(start, count, kind, group):
        some = pl.ds(start, count)
        return remote(
            turned.at[some], mirror.at[some], turn_send.at[kind], turn_recv.at[group],
            lax.rem(me + 1, n),
        )

    def first_quarter(m, which):
        c = 3 - m if which else m
        pl.when(has_up)(halo(1, m, which).wait_recv)
        pl.when(has_down)(halo(0, m, which).wait_recv)
        loop(NEAR // step, functools.partial(outer, c))

        def make_turn(t):
            s = c * per + lax.rem(me + t, per)
            turned[s] = turn(s)

        short(per, make_turn)

        def send_group(kind):
            def send(t):
                s = c * per + lax.rem(me + t, per)
                pl.when(s != me)(lambda: turn_copy(s, kind).start())

            short(per, send)

        pl.when(mine == c ^ 2)(lambda: send_group(0))
        pl.when(jnp.logical_and(mine != c ^ 2, mine != c ^ 3))(lambda: send_group(1))

    @pl.when(me < half)
    def _():
        for m in range(4):
            first_quarter(m, 1)

    @pl.when(me >= half)
    def _():
        for m in range(4):
            first_quarter(m, 0)

    def send_late(t):
        turn_copy((mine ^ 3) * per + lax.rem(me + t, per), 1).start()

    short(per, send_late)

    def edge(side, at, count):
        span = pl.ds(at, count)
        return remote(
            sym3.at[1, span], sym3.at[2 - 2 * side, span],
            edge_send.at[side], edge_recv.at[side], down if side else up,
        )

    even = me % 2 == 0

    def diagonal(r):
        return jnp.logical_or(r % 4 == 0, r % 4 == 3)

    def direct(s, r):
        near = (s >= half) == (r >= half)
        return jnp.logical_and(
            (s // 2) % 2 == (r // 2) % 2, jnp.logical_or(diagonal(r), near)
        )

    def direct_copy(s, r):
        return remote(
            staged.at[r], sym3.at[2 - 2 * (s % 2), me + 1],
            direct_send.at[r], edge_recv.at[s % 2], r,
        )

    def helped(s):
        r = s - 1 + 2 * (s % 2)
        return r, jnp.logical_and(jnp.logical_and(r >= 0, r < n), direct(me, r))

    def make_block(s, other):
        base = pl.multiple_of(s * FAR, FAR)
        own = [first[pl.ds(pl.multiple_of(base + i * width, FAR), FAR), :] for i in range(rows)]
        own = jnp.concatenate(own, axis=0)
        block = (0.5 * (own + other.astype(F32))).astype(BF16)
        sym3[1, s + 1] = block
        r, there = helped(s)

        @pl.when(there)
        def _():
            flip[...] = block.astype(F32)
            cols = [flip[pl.ds(j, rows, stride=FAR), :] for j in range(FAR)]
            turned_block = jnp.concatenate(cols, axis=0).astype(BF16)

            @pl.when(r == me)
            def _():
                sym3[2 - 2 * (s % 2), me + 1] = turned_block

            @pl.when(r != me)
            def _():
                staged[r] = turned_block
                direct_copy(s, r).start()

    def send_pairs(side, target, group):
        def send(p):
            s = group * per + 2 * p
            pl.when(jnp.logical_not(direct(s, target)))(edge(side, 1 + s, 2).start)

        short(per // 2, send)

    mirror[me] = turned[me]
    for far in range(4):
        group = mine ^ far
        count = per if far else per - 1
        turn_span(group * per, count, 1, group).wait_recv()

        def make(t):
            s = group * per + t
            make_block(s, mirror[s])

        short(per, make)

        @pl.when(even)
        def _():
            pl.when(has_up)(functools.partial(send_pairs, 0, up, group))
            edge(1, 1 + group * per, per).start()

        @pl.when(jnp.logical_not(even))
        def _():
            pl.when(has_down)(functools.partial(send_pairs, 1, down, group))
            edge(0, 1 + group * per, per).start()

    loads[2].wait()
    loads[3].wait()
    group = min(blocks, 16)
    high = group * tile

    def rows_of(strip, start):
        return sym3[strip, pl.ds(start, group)].reshape(high, chans)

    def product(strips, start):
        lhs = [rows_of(k, start + d) for k in strips for d in range(3)]
        rhs = [w2[k, d] for k in strips for d in range(3)]
        return jnp.dot(
            jnp.concatenate(lhs, axis=1), jnp.concatenate(rhs, axis=0),
            preferred_element_type=F32,
        )

    def middle(g):
        acc[pl.ds(pl.multiple_of(g * high, high), high)] = product((1,), g * group)

    loop(blocks // group, middle)

    def arrived(strip, count):
        there = has_down if strip else has_up
        pl.when(there)(edge(0 if strip else 1, 1, count).wait_recv)

    def finish(strip, g):
        total = acc[pl.ds(pl.multiple_of(g * high, high), high)] + product((strip,), g * group)
        second = jnp.maximum(total, 0.0).astype(BF16)
        side = jnp.dot(second, wp[...], preferred_element_type=F32)
        side = side.reshape(group, rows, FAR, chans)
        part = pl.ds(pl.multiple_of(g * group * FAR, group * FAR), group * FAR)
        for i in range(rows):
            base = xpad[NEAR + i, part].astype(F32)
            out_ref[i, part] = (base + side[:, i].reshape(group * FAR, chans)).astype(BF16)

    def last_strips(early, late):
        arrived(early, n)

        def add(g):
            span = pl.ds(pl.multiple_of(g * high, high), high)
            acc[span] = acc[span] + product((early,), g * group)

        loop(blocks // group, add)
        arrived(late, n - 1)
        loop(blocks // group, functools.partial(finish, late))

    pl.when(even)(lambda: last_strips(2, 0))
    pl.when(jnp.logical_not(even))(lambda: last_strips(0, 2))

    each_halo(range(4), lambda copy: copy.wait_send())
    turn_span(0, per, 0, 0).wait_send()
    turn_span(0, n - 1 - per, 1, 0).wait_send()

    def drain_pairs(side, target):
        skew = diagonal(target)
        pl.when(skew)(edge(side, 1, n // 2).wait_send)
        pl.when(jnp.logical_not(skew))(edge(side, 1, n - n // 4).wait_send)

    @pl.when(even)
    def _():
        pl.when(has_up)(functools.partial(drain_pairs, 0, up))
        edge(1, 1, n).wait_send()

    @pl.when(jnp.logical_not(even))
    def _():
        pl.when(has_down)(functools.partial(drain_pairs, 1, down))
        edge(0, 1, n).wait_send()

    def drain_direct(s):
        r, there = helped(s)
        pl.when(jnp.logical_and(there, r != me))(lambda: direct_copy(s, r).wait_send())

    loop(n, drain_direct)


def shards(contact_map, first_kernel, second_kernel, project_weight):
    args = (contact_map, first_kernel, second_kernel, project_weight)
    rows, width, chans = contact_map.shape
    n = lax.axis_size("row")
    assert rows == FAR and rows == 2 * NEAR and width == n * rows and n % 8 == 0
    tile = rows * FAR
    blocks = width // FAR
    moved = 9 * chans * chans * 4 + 4 * rows * width * chans
    return pl.pallas_call(
        functools.partial(block_kernel, n),
        out_shape=pltpu.VMEM(contact_map.shape, BF16),
        in_specs=[pl.BlockSpec(memory_space=pltpu.HBM)] * 4,
        out_specs=pl.BlockSpec(memory_space=pltpu.VMEM),
        scratch_shapes=[
            pltpu.VMEM((rows + 2 * NEAR, width, chans), BF16),
            pltpu.VMEM(first_kernel.shape, BF16),
            pltpu.VMEM(second_kernel.shape, BF16),
            pltpu.VMEM(project_weight.shape, BF16),
            pltpu.VMEM((rows * width, chans), F32),
            pltpu.VMEM((n, tile, chans), BF16),
            pltpu.VMEM((n, tile, chans), BF16),
            pltpu.VMEM((3, blocks + 2, tile, chans), BF16),
            pltpu.VMEM((rows * width, chans), F32),
            pltpu.VMEM((n, tile, chans), BF16),
            pltpu.VMEM((tile, chans), F32),
            pltpu.SemaphoreType.DMA((4,)),
            pltpu.SemaphoreType.DMA((2, 4)),
            pltpu.SemaphoreType.DMA((2, 4)),
            pltpu.SemaphoreType.DMA((2,)),
            pltpu.SemaphoreType.DMA((4,)),
            pltpu.SemaphoreType.DMA((2,)),
            pltpu.SemaphoreType.DMA((2,)),
            pltpu.SemaphoreType.DMA((n,)),
        ],
        compiler_params=pltpu.CompilerParams(
            collective_id=0, has_side_effects=True, vmem_limit_bytes=60 * 1024 * 1024
        ),
        cost_estimate=pl.CostEstimate(
            flops=2 * 19 * rows * width * chans * chans, bytes_accessed=moved, transcendentals=0
        ),
    )(*(pltpu.with_memory_space_constraint(x, pltpu.HBM) for x in args))


def solution(mesh):
    placed = (P(("win", "row"), None, None), P(), P(), P())
    return jax.shard_map(
        shards, mesh=mesh, in_specs=placed, out_specs=P(("win", "row"), None, None), check_vma=False
    )
```

```python
import functools

import jax
import jax.numpy as jnp
from jax import lax
from jax.experimental import pallas as pl
from jax.experimental.pallas import tpu as pltpu
from jax.sharding import PartitionSpec as P

NEAR = 4
FAR = 8
REACH = 16
BF16 = jnp.bfloat16
F32 = jnp.float32


def loop(count, body):
    if count == 1:
        body(0)
    else:
        lax.fori_loop(0, count, lambda i, c: (body(i), c)[1], 0)


def short(count, body):
    if count <= 4:
        for i in range(count):
            body(i)
    else:
        loop(count, body)


def block_kernel(
    n, x_hbm, k1_hbm, k2_hbm, pw_hbm, out_ref,
    xpad, w1, w2, wp, first, turned, mirror, sym3, acc, staged, flip,
    load_sem, halo_send, halo_recv, turn_send, turn_recv, edge_send, edge_recv, direct_send,
):
    rows, width, chans = x_hbm.shape
    tile = rows * FAR
    blocks = width // FAR
    me = lax.axis_index("row")
    up, down = me - 1, me + 1
    has_up, has_down = me > 0, me < n - 1

    loads = [
        pltpu.make_async_copy(x_hbm, xpad.at[pl.ds(NEAR, rows)], load_sem.at[0]),
        pltpu.make_async_copy(k1_hbm, w1, load_sem.at[1]),
        pltpu.make_async_copy(k2_hbm, w2, load_sem.at[2]),
        pltpu.make_async_copy(pw_hbm, wp, load_sem.at[3]),
    ]
    for load in loads:
        load.start()

    barrier = pltpu.get_barrier_semaphore()

    def greet(k):
        pl.semaphore_signal(
            barrier, inc=1, device_id={"row": lax.rem(me + k + 1, n)},
            device_id_type=pl.DeviceIdType.MESH,
        )

    loop(n - 1, greet)

    zeros = jnp.zeros((tile, chans), BF16)
    for strip in range(3):
        sym3[strip, 0] = zeros
        sym3[strip, blocks + 1] = zeros

    @pl.when(jnp.logical_not(has_up))
    def _():
        xpad[0:NEAR] = jnp.zeros((NEAR, width, chans), BF16)

        def clear(s):
            sym3[0, s + 1] = zeros

        loop(blocks, clear)

    @pl.when(jnp.logical_not(has_down))
    def _():
        xpad[NEAR + rows :] = jnp.zeros((NEAR, width, chans), BF16)

        def clear(s):
            sym3[2, s + 1] = zeros

        loop(blocks, clear)

    def remote(src, dst, send, recv, target):
        return pltpu.make_async_remote_copy(
            src_ref=src, dst_ref=dst, send_sem=send, recv_sem=recv,
            device_id={"row": target}, device_id_type=pl.DeviceIdType.MESH,
        )

    half = n // 2
    per = n // 4
    mine = me // per
    keep = width // 4
    edges = [0] + [c * keep + REACH for c in (1, 2, 3)] + [width]
    rising = [(edges[m], edges[m + 1] - edges[m]) for m in range(4)]
    falling = [(width - start - size, size) for start, size in rising]
    parts = (rising, falling)

    def halo(side, m, which):
        start, size = parts[which][m]
        cols = pl.ds(start, size)
        if side == 0:
            src, dst, target = pl.ds(0, NEAR), pl.ds(NEAR + rows, NEAR), up
        else:
            src, dst, target = pl.ds(rows - NEAR, NEAR), pl.ds(0, NEAR), down
        return remote(
            x_hbm.at[src, cols], xpad.at[dst, cols],
            halo_send.at[side, m], halo_recv.at[side, m], target,
        )

    def each_halo(parts_of, visit):
        for which in (0, 1):
            for side, there, target in ((0, has_up, up), (1, has_down, down)):
                wanted = (target >= half) if which == 0 else (target < half)

                @pl.when(jnp.logical_and(there, wanted))
                def _():
                    for m in parts_of:
                        visit(halo(side, m, which))

    pl.semaphore_wait(barrier, n - 1)

    each_halo((0,), lambda copy: copy.start())

    loads[0].wait()
    loads[1].wait()

    step = max(1, min(NEAR, 512 // width))

    def taps(strips, kinds, wide):
        depth = step * wide
        lhs = [strip.reshape(depth, chans) for strip in strips]
        lhs = jnp.concatenate(lhs, axis=1) if len(lhs) > 1 else lhs[0]
        rhs = [jnp.concatenate([w1[k, d] for d in range(3)], axis=1) for k in kinds]
        rhs = jnp.concatenate(rhs, axis=0) if len(rhs) > 1 else rhs[0]
        prod = jnp.dot(lhs, rhs, preferred_element_type=F32)
        column = lax.broadcasted_iota(jnp.int32, (step, wide, chans), 1).reshape(depth, chans)
        left = pltpu.roll(prod[:, :chans], NEAR, 0)
        right = pltpu.roll(prod[:, 2 * chans :], depth - NEAR, 0)
        return (
            prod[:, chans : 2 * chans]
            + jnp.where(column >= NEAR, left, 0.0)
            + jnp.where(column < wide - NEAR, right, 0.0)
        )

    def inner(shift, kinds, g):
        a = g * step
        near, mid = xpad[pl.ds(NEAR + a, step)], xpad[pl.ds(2 * NEAR + a, step)]
        row = shift + a
        first[pl.ds(pl.multiple_of(row * width, width), step * width)] = taps(
            [near, mid], kinds, width
        )

    loop(NEAR // step, functools.partial(inner, 0, (1, 2)))
    each_halo((1,), lambda copy: copy.start())
    loop(NEAR // step, functools.partial(inner, NEAR, (0, 1)))
    each_halo((2, 3), lambda copy: copy.start())

    def outer(c, g):
        a = g * step
        start = max(0, c * keep - REACH)
        off = c * keep - start
        wide = min(width, (c + 1) * keep + REACH) - start
        for row, source, kind in ((a, a, 0), (NEAR + a, rows + NEAR + a, 2)):
            extra = taps([xpad[pl.ds(source, step), pl.ds(start, wide)]], (kind,), wide)
            for i in range(step):
                span = pl.ds(pl.multiple_of((row + i) * width + c * keep, keep), keep)
                total = first[span] + extra[i * wide + off : i * wide + off + keep]
                first[span] = jnp.maximum(total, 0.0).astype(BF16).astype(F32)

    def turn(s):
        base = pl.multiple_of(s * FAR, FAR)
        cols = [first[pl.ds(base + j, rows, stride=width), :] for j in range(FAR)]
        return jnp.concatenate(cols, axis=0).astype(BF16)

    def turn_copy(s, kind):
        return remote(
            turned.at[s], mirror.at[me], turn_send.at[kind], turn_recv.at[mine], s
        )

    def turn_span(start, count, kind, group):
        some = pl.ds(start, count)
        return remote(
            turned.at[some], mirror.at[some], turn_send.at[kind], turn_recv.at[group],
            lax.rem(me + 1, n),
        )

    def first_quarter(m, which):
        c = 3 - m if which else m
        pl.when(has_up)(halo(1, m, which).wait_recv)
        pl.when(has_down)(halo(0, m, which).wait_recv)
        loop(NEAR // step, functools.partial(outer, c))

        def make_turn(t):
            s = c * per + lax.rem(me + t, per)
            turned[s] = turn(s)

        short(per, make_turn)

        def send_group(kind):
            def send(t):
                s = c * per + lax.rem(me + t, per)
                pl.when(s != me)(lambda: turn_copy(s, kind).start())

            short(per, send)

        pl.when(mine == c ^ 2)(lambda: send_group(0))
        pl.when(jnp.logical_and(mine != c ^ 2, mine != c ^ 3))(lambda: send_group(1))

    @pl.when(me < half)
    def _():
        for m in range(4):
            first_quarter(m, 1)

    @pl.when(me >= half)
    def _():
        for m in range(4):
            first_quarter(m, 0)

    def send_late(t):
        turn_copy((mine ^ 3) * per + lax.rem(me + t, per), 1).start()

    short(per, send_late)

    def edge(side, at, count):
        span = pl.ds(at, count)
        return remote(
            sym3.at[1, span], sym3.at[2 - 2 * side, span],
            edge_send.at[side], edge_recv.at[side], down if side else up,
        )

    even = me % 2 == 0

    def diagonal(r):
        return jnp.logical_or(r % 4 == 0, r % 4 == 3)

    def direct(s, r):
        near = (s >= half) == (r >= half)
        return jnp.logical_and(
            (s // 2) % 2 == (r // 2) % 2, jnp.logical_or(diagonal(r), near)
        )

    def direct_copy(s, r):
        return remote(
            staged.at[r], sym3.at[2 - 2 * (s % 2), me + 1],
            direct_send.at[r], edge_recv.at[s % 2], r,
        )

    def helped(s):
        r = s - 1 + 2 * (s % 2)
        return r, jnp.logical_and(jnp.logical_and(r >= 0, r < n), direct(me, r))

    def make_block(s, other):
        base = pl.multiple_of(s * FAR, FAR)
        own = [first[pl.ds(pl.multiple_of(base + i * width, FAR), FAR), :] for i in range(rows)]
        own = jnp.concatenate(own, axis=0)
        block = (0.5 * (own + other.astype(F32))).astype(BF16)
        sym3[1, s + 1] = block
        r, there = helped(s)

        @pl.when(there)
        def _():
            flip[...] = block.astype(F32)
            cols = [flip[pl.ds(j, rows, stride=FAR), :] for j in range(FAR)]
            turned_block = jnp.concatenate(cols, axis=0).astype(BF16)

            @pl.when(r == me)
            def _():
                sym3[2 - 2 * (s % 2), me + 1] = turned_block

            @pl.when(r != me)
            def _():
                staged[r] = turned_block
                direct_copy(s, r).start()

    def send_pairs(side, target, group):
        def send(p):
            s = group * per + 2 * p
            pl.when(jnp.logical_not(direct(s, target)))(edge(side, 1 + s, 2).start)

        short(per // 2, send)

    mirror[me] = turned[me]
    for far in range(4):
        group = mine ^ far
        count = per if far else per - 1
        turn_span(group * per, count, 1, group).wait_recv()

        def make(t):
            s = group * per + t
            make_block(s, mirror[s])

        short(per, make)

        @pl.when(even)
        def _():
            pl.when(has_up)(functools.partial(send_pairs, 0, up, group))
            edge(1, 1 + group * per, per).start()

        @pl.when(jnp.logical_not(even))
        def _():
            pl.when(has_down)(functools.partial(send_pairs, 1, down, group))
            edge(0, 1 + group * per, per).start()

    loads[2].wait()
    loads[3].wait()
    group = min(blocks, 16)
    high = group * tile

    def rows_of(strip, start):
        return sym3[strip, pl.ds(start, group)].reshape(high, chans)

    def product(strips, start):
        lhs = [rows_of(k, start + d) for k in strips for d in range(3)]
        rhs = [w2[k, d] for k in strips for d in range(3)]
        return jnp.dot(
            jnp.concatenate(lhs, axis=1), jnp.concatenate(rhs, axis=0),
            preferred_element_type=F32,
        )

    def middle(g):
        acc[pl.ds(pl.multiple_of(g * high, high), high)] = product((1,), g * group)

    loop(blocks // group, middle)

    def arrived(strip, count):
        there = has_down if strip else has_up
        pl.when(there)(edge(0 if strip else 1, 1, count).wait_recv)

    def finish(strip, g):
        total = acc[pl.ds(pl.multiple_of(g * high, high), high)] + product((strip,), g * group)
        second = jnp.maximum(total, 0.0).astype(BF16)
        side = jnp.dot(second, wp[...], preferred_element_type=F32)
        side = side.reshape(group, rows, FAR, chans)
        part = pl.ds(pl.multiple_of(g * group * FAR, group * FAR), group * FAR)
        for i in range(rows):
            base = xpad[NEAR + i, part].astype(F32)
            out_ref[i, part] = (base + side[:, i].reshape(group * FAR, chans)).astype(BF16)

    def early_strip(strip):
        arrived(strip, n)

        def add(g):
            span = pl.ds(pl.multiple_of(g * high, high), high)
            acc[span] = acc[span] + product((strip,), g * group)

        loop(blocks // group, add)

    pl.when(even)(lambda: early_strip(2))
    pl.when(jnp.logical_not(even))(lambda: early_strip(0))

    each_halo(range(4), lambda copy: copy.wait_send())
    turn_span(0, per, 0, 0).wait_send()
    turn_span(0, n - 1 - per, 1, 0).wait_send()

    def drain_pairs(side, target):
        skew = diagonal(target)
        pl.when(skew)(edge(side, 1, n // 2).wait_send)
        pl.when(jnp.logical_not(skew))(edge(side, 1, n - n // 4).wait_send)

    @pl.when(even)
    def _():
        pl.when(has_up)(functools.partial(drain_pairs, 0, up))
        edge(1, 1, n).wait_send()

    @pl.when(jnp.logical_not(even))
    def _():
        pl.when(has_down)(functools.partial(drain_pairs, 1, down))
        edge(0, 1, n).wait_send()

    def drain_direct(s):
        r, there = helped(s)
        pl.when(jnp.logical_and(there, r != me))(lambda: direct_copy(s, r).wait_send())

    loop(n, drain_direct)

    def late_strip(strip):
        arrived(strip, n - 1)
        loop(blocks // group, functools.partial(finish, strip))

    pl.when(even)(lambda: late_strip(0))
    pl.when(jnp.logical_not(even))(lambda: late_strip(2))


def shards(contact_map, first_kernel, second_kernel, project_weight):
    args = (contact_map, first_kernel, second_kernel, project_weight)
    rows, width, chans = contact_map.shape
    n = lax.axis_size("row")
    assert rows == FAR and rows == 2 * NEAR and width == n * rows and n % 8 == 0
    tile = rows * FAR
    blocks = width // FAR
    moved = 9 * chans * chans * 4 + 4 * rows * width * chans
    return pl.pallas_call(
        functools.partial(block_kernel, n),
        out_shape=pltpu.VMEM(contact_map.shape, BF16),
        in_specs=[pl.BlockSpec(memory_space=pltpu.HBM)] * 4,
        out_specs=pl.BlockSpec(memory_space=pltpu.VMEM),
        scratch_shapes=[
            pltpu.VMEM((rows + 2 * NEAR, width, chans), BF16),
            pltpu.VMEM(first_kernel.shape, BF16),
            pltpu.VMEM(second_kernel.shape, BF16),
            pltpu.VMEM(project_weight.shape, BF16),
            pltpu.VMEM((rows * width, chans), F32),
            pltpu.VMEM((n, tile, chans), BF16),
            pltpu.VMEM((n, tile, chans), BF16),
            pltpu.VMEM((3, blocks + 2, tile, chans), BF16),
            pltpu.VMEM((rows * width, chans), F32),
            pltpu.VMEM((n, tile, chans), BF16),
            pltpu.VMEM((tile, chans), F32),
            pltpu.SemaphoreType.DMA((4,)),
            pltpu.SemaphoreType.DMA((2, 4)),
            pltpu.SemaphoreType.DMA((2, 4)),
            pltpu.SemaphoreType.DMA((2,)),
            pltpu.SemaphoreType.DMA((4,)),
            pltpu.SemaphoreType.DMA((2,)),
            pltpu.SemaphoreType.DMA((2,)),
            pltpu.SemaphoreType.DMA((n,)),
        ],
        compiler_params=pltpu.CompilerParams(
            collective_id=0, has_side_effects=True, vmem_limit_bytes=60 * 1024 * 1024
        ),
        cost_estimate=pl.CostEstimate(
            flops=2 * 19 * rows * width * chans * chans, bytes_accessed=moved, transcendentals=0
        ),
    )(*(pltpu.with_memory_space_constraint(x, pltpu.HBM) for x in args))


def solution(mesh):
    placed = (P(("win", "row"), None, None), P(), P(), P())
    return jax.shard_map(
        shards, mesh=mesh, in_specs=placed, out_specs=P(("win", "row"), None, None), check_vma=False
    )
```

```python
import functools

import jax
import jax.numpy as jnp
from jax import lax
from jax.experimental import pallas as pl
from jax.experimental.pallas import tpu as pltpu
from jax.sharding import PartitionSpec as P

NEAR = 4
FAR = 8
REACH = 16
BF16 = jnp.bfloat16
F32 = jnp.float32


def loop(count, body):
    if count == 1:
        body(0)
    else:
        lax.fori_loop(0, count, lambda i, c: (body(i), c)[1], 0)


def short(count, body):
    if count <= 4:
        for i in range(count):
            body(i)
    else:
        loop(count, body)


def block_kernel(
    n, x_hbm, k1_hbm, k2_hbm, pw_hbm, out_ref,
    xpad, w1, w2, wp, first, turned, mirror, sym3, acc, staged, flip,
    load_sem, halo_send, halo_recv, turn_send, turn_recv, edge_send, edge_recv, direct_send,
):
    rows, width, chans = x_hbm.shape
    tile = rows * FAR
    blocks = width // FAR
    me = lax.axis_index("row")
    up, down = me - 1, me + 1
    has_up, has_down = me > 0, me < n - 1

    loads = [
        pltpu.make_async_copy(x_hbm, xpad.at[pl.ds(NEAR, rows)], load_sem.at[0]),
        pltpu.make_async_copy(k1_hbm, w1, load_sem.at[1]),
        pltpu.make_async_copy(k2_hbm, w2, load_sem.at[2]),
        pltpu.make_async_copy(pw_hbm, wp, load_sem.at[3]),
    ]
    for load in loads:
        load.start()

    barrier = pltpu.get_barrier_semaphore()

    def greet(k):
        pl.semaphore_signal(
            barrier, inc=1, device_id={"row": lax.rem(me + k + 1, n)},
            device_id_type=pl.DeviceIdType.MESH,
        )

    loop(n - 1, greet)

    zeros = jnp.zeros((tile, chans), BF16)
    for strip in range(3):
        sym3[strip, 0] = zeros
        sym3[strip, blocks + 1] = zeros

    @pl.when(jnp.logical_not(has_up))
    def _():
        xpad[0:NEAR] = jnp.zeros((NEAR, width, chans), BF16)

        def clear(s):
            sym3[0, s + 1] = zeros

        loop(blocks, clear)

    @pl.when(jnp.logical_not(has_down))
    def _():
        xpad[NEAR + rows :] = jnp.zeros((NEAR, width, chans), BF16)

        def clear(s):
            sym3[2, s + 1] = zeros

        loop(blocks, clear)

    def remote(src, dst, send, recv, target):
        return pltpu.make_async_remote_copy(
            src_ref=src, dst_ref=dst, send_sem=send, recv_sem=recv,
            device_id={"row": target}, device_id_type=pl.DeviceIdType.MESH,
        )

    half = n // 2
    per = n // 4
    mine = me // per
    keep = width // 4
    edges = [0] + [c * keep + REACH for c in (1, 2, 3)] + [width]
    rising = [(edges[m], edges[m + 1] - edges[m]) for m in range(4)]
    falling = [(width - start - size, size) for start, size in rising]
    parts = (rising, falling)

    def halo(side, m, which):
        start, size = parts[which][m]
        cols = pl.ds(start, size)
        if side == 0:
            src, dst, target = pl.ds(0, NEAR), pl.ds(NEAR + rows, NEAR), up
        else:
            src, dst, target = pl.ds(rows - NEAR, NEAR), pl.ds(0, NEAR), down
        return remote(
            x_hbm.at[src, cols], xpad.at[dst, cols],
            halo_send.at[side, m], halo_recv.at[side, m], target,
        )

    def each_halo(parts_of, visit):
        for which in (0, 1):
            for side, there, target in ((0, has_up, up), (1, has_down, down)):
                wanted = (target >= half) if which == 0 else (target < half)

                @pl.when(jnp.logical_and(there, wanted))
                def _():
                    for m in parts_of:
                        visit(halo(side, m, which))

    pl.semaphore_wait(barrier, n - 1)

    each_halo((0,), lambda copy: copy.start())

    loads[0].wait()
    loads[1].wait()

    step = max(1, min(NEAR, 512 // width))

    def taps(strips, kinds, wide):
        depth = step * wide
        lhs = [strip.reshape(depth, chans) for strip in strips]
        lhs = jnp.concatenate(lhs, axis=1) if len(lhs) > 1 else lhs[0]
        rhs = [jnp.concatenate([w1[k, d] for d in range(3)], axis=1) for k in kinds]
        rhs = jnp.concatenate(rhs, axis=0) if len(rhs) > 1 else rhs[0]
        prod = jnp.dot(lhs, rhs, preferred_element_type=F32)
        column = lax.broadcasted_iota(jnp.int32, (step, wide, chans), 1).reshape(depth, chans)
        left = pltpu.roll(prod[:, :chans], NEAR, 0)
        right = pltpu.roll(prod[:, 2 * chans :], depth - NEAR, 0)
        return (
            prod[:, chans : 2 * chans]
            + jnp.where(column >= NEAR, left, 0.0)
            + jnp.where(column < wide - NEAR, right, 0.0)
        )

    def inner(shift, kinds, g):
        a = g * step
        near, mid = xpad[pl.ds(NEAR + a, step)], xpad[pl.ds(2 * NEAR + a, step)]
        row = shift + a
        first[pl.ds(pl.multiple_of(row * width, width), step * width)] = taps(
            [near, mid], kinds, width
        )

    loop(NEAR // step, functools.partial(inner, 0, (1, 2)))
    each_halo((1,), lambda copy: copy.start())
    loop(NEAR // step, functools.partial(inner, NEAR, (0, 1)))
    each_halo((2, 3), lambda copy: copy.start())

    def outer(c, g):
        a = g * step
        start = max(0, c * keep - REACH)
        off = c * keep - start
        wide = min(width, (c + 1) * keep + REACH) - start
        for row, source, kind in ((a, a, 0), (NEAR + a, rows + NEAR + a, 2)):
            extra = taps([xpad[pl.ds(source, step), pl.ds(start, wide)]], (kind,), wide)
            for i in range(step):
                span = pl.ds(pl.multiple_of((row + i) * width + c * keep, keep), keep)
                total = first[span] + extra[i * wide + off : i * wide + off + keep]
                first[span] = jnp.maximum(total, 0.0).astype(BF16).astype(F32)

    def turn(s):
        base = pl.multiple_of(s * FAR, FAR)
        cols = [first[pl.ds(base + j, rows, stride=width), :] for j in range(FAR)]
        return jnp.concatenate(cols, axis=0).astype(BF16)

    def turn_copy(s, kind):
        return remote(
            turned.at[s], mirror.at[me], turn_send.at[kind], turn_recv.at[mine], s
        )

    def turn_span(start, count, kind, group):
        some = pl.ds(start, count)
        return remote(
            turned.at[some], mirror.at[some], turn_send.at[kind], turn_recv.at[group],
            lax.rem(me + 1, n),
        )

    def first_quarter(m, which):
        c = 3 - m if which else m
        pl.when(has_up)(halo(1, m, which).wait_recv)
        pl.when(has_down)(halo(0, m, which).wait_recv)
        loop(NEAR // step, functools.partial(outer, c))

        def make_turn(t):
            s = c * per + lax.rem(me + t, per)
            turned[s] = turn(s)

        short(per, make_turn)

        def send_group(kind):
            def send(t):
                s = c * per + lax.rem(me + t, per)
                pl.when(s != me)(lambda: turn_copy(s, kind).start())

            short(per, send)

        pl.when(mine == c ^ 2)(lambda: send_group(0))
        pl.when(jnp.logical_and(mine != c ^ 2, mine != c ^ 3))(lambda: send_group(1))

    @pl.when(me < half)
    def _():
        for m in range(4):
            first_quarter(m, 1)

    @pl.when(me >= half)
    def _():
        for m in range(4):
            first_quarter(m, 0)

    def send_late(t):
        turn_copy((mine ^ 3) * per + lax.rem(me + t, per), 1).start()

    short(per, send_late)

    def edge(side, at, count):
        span = pl.ds(at, count)
        return remote(
            sym3.at[1, span], sym3.at[2 - 2 * side, span],
            edge_send.at[side], edge_recv.at[side], down if side else up,
        )

    even = me % 2 == 0

    def direct(s, r):
        return (s // 2) % 2 == (r // 2) % 2

    def direct_copy(s, r):
        return remote(
            staged.at[r], sym3.at[2 - 2 * (s % 2), me + 1],
            direct_send.at[r], edge_recv.at[s % 2], r,
        )

    def helped(s):
        r = s - 1 + 2 * (s % 2)
        return r, jnp.logical_and(jnp.logical_and(r >= 0, r < n), direct(me, r))

    def make_block(s, other):
        base = pl.multiple_of(s * FAR, FAR)
        own = [first[pl.ds(pl.multiple_of(base + i * width, FAR), FAR), :] for i in range(rows)]
        own = jnp.concatenate(own, axis=0)
        block = (0.5 * (own + other.astype(F32))).astype(BF16)
        sym3[1, s + 1] = block
        r, there = helped(s)

        @pl.when(there)
        def _():
            flip[...] = block.astype(F32)
            cols = [flip[pl.ds(j, rows, stride=FAR), :] for j in range(FAR)]
            turned_block = jnp.concatenate(cols, axis=0).astype(BF16)

            @pl.when(r == me)
            def _():
                sym3[2 - 2 * (s % 2), me + 1] = turned_block

            @pl.when(r != me)
            def _():
                staged[r] = turned_block
                direct_copy(s, r).start()

    def send_pairs(side, target, group):
        def send(p):
            s = group * per + 2 * p
            pl.when(jnp.logical_not(direct(s, target)))(edge(side, 1 + s, 2).start)

        short(per // 2, send)

    mirror[me] = turned[me]
    for far in range(4):
        group = mine ^ far
        count = per if far else per - 1
        turn_span(group * per, count, 1, group).wait_recv()

        def make(t):
            s = group * per + t
            make_block(s, mirror[s])

        short(per, make)

        @pl.when(even)
        def _():
            pl.when(has_up)(functools.partial(send_pairs, 0, up, group))
            edge(1, 1 + group * per, per).start()

        @pl.when(jnp.logical_not(even))
        def _():
            pl.when(has_down)(functools.partial(send_pairs, 1, down, group))
            edge(0, 1 + group * per, per).start()

    loads[2].wait()
    loads[3].wait()
    group = min(blocks, 16)
    high = group * tile

    def rows_of(strip, start):
        return sym3[strip, pl.ds(start, group)].reshape(high, chans)

    def product(strips, start):
        lhs = [rows_of(k, start + d) for k in strips for d in range(3)]
        rhs = [w2[k, d] for k in strips for d in range(3)]
        return jnp.dot(
            jnp.concatenate(lhs, axis=1), jnp.concatenate(rhs, axis=0),
            preferred_element_type=F32,
        )

    def middle(g):
        acc[pl.ds(pl.multiple_of(g * high, high), high)] = product((1,), g * group)

    loop(blocks // group, middle)

    def arrived(strip, count):
        there = has_down if strip else has_up
        pl.when(there)(edge(0 if strip else 1, 1, count).wait_recv)

    def finish(strip, g):
        total = acc[pl.ds(pl.multiple_of(g * high, high), high)] + product((strip,), g * group)
        second = jnp.maximum(total, 0.0).astype(BF16)
        side = jnp.dot(second, wp[...], preferred_element_type=F32)
        side = side.reshape(group, rows, FAR, chans)
        part = pl.ds(pl.multiple_of(g * group * FAR, group * FAR), group * FAR)
        for i in range(rows):
            base = xpad[NEAR + i, part].astype(F32)
            out_ref[i, part] = (base + side[:, i].reshape(group * FAR, chans)).astype(BF16)

    def early_strip(strip):
        arrived(strip, n)

        def add(g):
            span = pl.ds(pl.multiple_of(g * high, high), high)
            acc[span] = acc[span] + product((strip,), g * group)

        loop(blocks // group, add)

    pl.when(even)(lambda: early_strip(2))
    pl.when(jnp.logical_not(even))(lambda: early_strip(0))

    each_halo(range(4), lambda copy: copy.wait_send())
    turn_span(0, per, 0, 0).wait_send()
    turn_span(0, n - 1 - per, 1, 0).wait_send()

    def drain_pairs(side, target):
        edge(side, 1, n // 2).wait_send()

    @pl.when(even)
    def _():
        pl.when(has_up)(functools.partial(drain_pairs, 0, up))
        edge(1, 1, n).wait_send()

    @pl.when(jnp.logical_not(even))
    def _():
        pl.when(has_down)(functools.partial(drain_pairs, 1, down))
        edge(0, 1, n).wait_send()

    def drain_direct(s):
        r, there = helped(s)
        pl.when(jnp.logical_and(there, r != me))(lambda: direct_copy(s, r).wait_send())

    loop(n, drain_direct)

    def late_strip(strip):
        arrived(strip, n - 1)
        loop(blocks // group, functools.partial(finish, strip))

    pl.when(even)(lambda: late_strip(0))
    pl.when(jnp.logical_not(even))(lambda: late_strip(2))


def shards(contact_map, first_kernel, second_kernel, project_weight):
    args = (contact_map, first_kernel, second_kernel, project_weight)
    rows, width, chans = contact_map.shape
    n = lax.axis_size("row")
    assert rows == FAR and rows == 2 * NEAR and width == n * rows and n % 8 == 0
    tile = rows * FAR
    blocks = width // FAR
    moved = 9 * chans * chans * 4 + 4 * rows * width * chans
    return pl.pallas_call(
        functools.partial(block_kernel, n),
        out_shape=pltpu.VMEM(contact_map.shape, BF16),
        in_specs=[pl.BlockSpec(memory_space=pltpu.HBM)] * 4,
        out_specs=pl.BlockSpec(memory_space=pltpu.VMEM),
        scratch_shapes=[
            pltpu.VMEM((rows + 2 * NEAR, width, chans), BF16),
            pltpu.VMEM(first_kernel.shape, BF16),
            pltpu.VMEM(second_kernel.shape, BF16),
            pltpu.VMEM(project_weight.shape, BF16),
            pltpu.VMEM((rows * width, chans), F32),
            pltpu.VMEM((n, tile, chans), BF16),
            pltpu.VMEM((n, tile, chans), BF16),
            pltpu.VMEM((3, blocks + 2, tile, chans), BF16),
            pltpu.VMEM((rows * width, chans), F32),
            pltpu.VMEM((n, tile, chans), BF16),
            pltpu.VMEM((tile, chans), F32),
            pltpu.SemaphoreType.DMA((4,)),
            pltpu.SemaphoreType.DMA((2, 4)),
            pltpu.SemaphoreType.DMA((2, 4)),
            pltpu.SemaphoreType.DMA((2,)),
            pltpu.SemaphoreType.DMA((4,)),
            pltpu.SemaphoreType.DMA((2,)),
            pltpu.SemaphoreType.DMA((2,)),
            pltpu.SemaphoreType.DMA((n,)),
        ],
        compiler_params=pltpu.CompilerParams(
            collective_id=0, has_side_effects=True, vmem_limit_bytes=60 * 1024 * 1024
        ),
        cost_estimate=pl.CostEstimate(
            flops=2 * 19 * rows * width * chans * chans, bytes_accessed=moved, transcendentals=0
        ),
    )(*(pltpu.with_memory_space_constraint(x, pltpu.HBM) for x in args))


def solution(mesh):
    placed = (P(("win", "row"), None, None), P(), P(), P())
    return jax.shard_map(
        shards, mesh=mesh, in_specs=placed, out_specs=P(("win", "row"), None, None), check_vma=False
    )
```
